256 devices in a mesh: blk: 8 (over x, core), tile: 32 (over y, z).
Axes of the slice: x: 4, y: 4, z: 8, core: 2. Of those that a mesh axis runs over, the one named last changes fastest.
Arguments:
- facet_temp: float32 [48, 32, 5120], P(None, 'tile', 'blk'), may hold values from 0.85 to 1.15
- emissivity: float32 [32, 5120], P('tile', 'blk'), may hold values from 0.2 to 0.95
- longwave_in: float32 [48, 32, 5120], P(None, 'tile', 'blk'), may hold values from 0.5 to 1.2
- albedo: float32 [32, 5120], P('tile', 'blk'), may hold values from 0.1 to 0.6
- shortwave_in: float32 [48, 32, 5120], P(None, 'tile', 'blk'), may hold values from 0.05 to 3
- dir_share: bfloat16 [6, 32, 5120], P(None, 'tile', 'blk'), may hold values from 0.049804688 to 1
- view_blocks: bfloat16 [8, 32, 32, 8, 128, 128], P('blk', 'tile'), may hold values from 0 to 1, as said below
- vis_list: int32 [2048, 32], P(('blk', 'tile')), may hold values from 0 to 39
- vis_mask: int32 [2048, 32], P(('blk', 'tile')), may hold values from 0 to 1, as said below
- vis_source: int32 [2048, 32], P(('blk', 'tile')), may hold values from 0 to 31, as said below
Outputs:
- directional_flux: float32 [6, 2, 48, 262144], P(None, None, None, ('blk', 'tile'))
- radiant_temp: float32 [48, 262144], P(None, ('blk', 'tile'))
The draws below stay inside these ranges and needn't reach their ends.
Inputs may be any that keep to these rules, and one draw needn't show every extreme that they name: `vis_mask`: every point tile has at least one set slot. In every index of blk at least one owner (the 8 tiles of one device) has all slots of all its tiles set. Among the set entries of one owner, each tracer is named at most 8 times. The view block of a set entry lies in view_blocks at [b, vis_source, t, slot] as in the reference program; unset entries name any tracer. `view_blocks`: positive view factors.
All inputs are finite; a program needn't handle non-finite values.
Results may differ from the reference program's by a relative error of at most 0.0003.
Values may be sent and summed in bfloat16 or wider, within the bound.
A program may use at most 128 MiB of HBM per device.

```python
import math
import jax
import jax.numpy as jnp
from jax import lax

TR = 128
FR = 128
DIRS = 6
BANDS = 2
HOURS = 48
K = 32
TPD = 8
CAP = 8
STRIPS = 32
NBS = 40
SF = 5120
TILES = 2048
N_BLK = 8
N_TILE = 32


def visibility(key):
    tile_total = TPD * N_BLK * N_TILE
    owner_total = N_BLK * N_TILE
    k_heavy, k_coin, k_force, k_perm, k_free = jax.random.split(jax.random.fold_in(key, 7), 5)
    heavy_owner = jax.random.randint(k_heavy, (N_BLK,), 0, N_TILE)
    coin_flip = jax.random.randint(k_coin, (tile_total, K), 0, 3) == 0
    forced = jax.random.randint(k_force, (tile_total,), 0, K)
    slot_ids = jnp.arange(K, dtype=jnp.int32)
    owner_ids = jnp.arange(tile_total, dtype=jnp.int32) // TPD
    is_heavy = heavy_owner[owner_ids // N_TILE] == owner_ids % N_TILE
    set_mask = coin_flip | (slot_ids[None, :] == forced[:, None]) | is_heavy[:, None]
    set_mask = set_mask.astype(jnp.int32).reshape(owner_total, TPD * K)
    set_order = jnp.cumsum(set_mask, axis=1) - set_mask
    tracer_perm = jax.vmap(lambda subkey: jax.random.permutation(subkey, N_TILE))(jax.random.split(k_perm, owner_total)).astype(jnp.int32)
    chosen = jnp.take_along_axis(tracer_perm, set_order % N_TILE, axis=1)
    free_source = jax.random.randint(k_free, (owner_total, TPD * K), 0, N_TILE)
    source = jnp.where(set_mask == 1, chosen, free_source).astype(jnp.int32)
    return (set_mask.reshape(tile_total, K), source.reshape(tile_total, K))


def draw_vis_mask(key, part):
    return visibility(key)[0]


def draw_vis_source(key, part):
    return visibility(key)[1]


def draw_view_blocks(key, part):
    full_shape = (N_BLK, N_TILE, N_TILE, CAP, FR, TR)
    view_scale = 1.0 / (K * FR)
    subkey = jax.random.fold_in(key, 11)
    k_entry = jax.random.fold_in(subkey, 0)
    values = jnp.exp(jax.random.uniform(k_entry, full_shape, jnp.float32, -1.15, 1.15))
    return (view_scale * values).astype(jnp.bfloat16)


def plant(values, own_key, low, top_value):
    place = [jax.random.randint(jax.random.fold_in(own_key, axis), (), 0, length) for axis, length in enumerate(values.shape)]
    main_axis = values.shape.index(max(values.shape))
    neighbour = place[:main_axis] + [(place[main_axis] + 1) % values.shape[main_axis]] + place[main_axis + 1:]
    return values.at[tuple(place)].set(low).at[tuple(neighbour)].set(top_value)


def block_levels(key, extent, pieces, low, top_value):
    def one(axis_at, shards_of):
        draws = jax.random.uniform(jax.random.fold_in(jax.random.fold_in(key, 6), axis_at), (shards_of,), jnp.float32, low / len(pieces), top_value / len(pieces))
        return jnp.repeat(jnp.exp(draws), extent[axis_at] // shards_of).reshape((-1,) + (1,) * (len(extent) - axis_at - 1))

    gain = one(*pieces[0])
    for cut in pieces[1:]:
        gain = gain * one(*cut)
    return gain


def setup_inputs(seed: int = 0) -> dict:
    key_list = jax.random.split(jax.random.key(seed), 11)
    facet_temp = jnp.clip(0.85 + 0.29999995 * jax.random.uniform(key_list[0], (HOURS, STRIPS, SF), jnp.float32) ** block_levels(key_list[0], (HOURS, STRIPS, SF), ((1, 32), (2, 8)), -0.2, 0.2), 0.85, 1.15)
    emissivity = jnp.clip(0.2 + 0.75 * jax.random.uniform(key_list[1], (STRIPS, SF), jnp.float32) ** block_levels(key_list[1], (STRIPS, SF), ((0, 32), (1, 8)), -0.2, 0.2), 0.2, 0.95)
    longwave_in = jnp.clip(0.5 + 0.70000005 * jax.random.uniform(key_list[2], (HOURS, STRIPS, SF), jnp.float32) ** block_levels(key_list[2], (HOURS, STRIPS, SF), ((1, 32), (2, 8)), -0.2, 0.2), 0.5, 1.2)
    albedo = jnp.clip(0.1 + 0.5 * jax.random.uniform(key_list[3], (STRIPS, SF), jnp.float32) ** block_levels(key_list[3], (STRIPS, SF), ((0, 32), (1, 8)), -0.2, 0.2), 0.1, 0.6)
    shortwave_in = jnp.clip(jnp.exp(math.log(3.0) - 4.0943445 * jax.random.uniform(key_list[4], (HOURS, STRIPS, SF), jnp.float32) ** block_levels(key_list[4], (HOURS, STRIPS, SF), ((1, 32), (2, 8)), -0.2, 0.2)), 0.05, 3.0)
    dir_share = jnp.clip(0.049804688 + 0.9501953 * jax.random.uniform(key_list[5], (DIRS, STRIPS, SF), jnp.float32) ** block_levels(key_list[5], (DIRS, STRIPS, SF), ((1, 32), (2, 8)), -0.2, 0.2), 0.049804688, 1.0).astype(jnp.bfloat16)
    view_blocks = draw_view_blocks(jax.random.fold_in(key_list[10], 71), 0)
    vis_list = plant(jax.random.randint(key_list[7], (TILES, K), 0, NBS), jax.random.fold_in(key_list[7], 1), 0, NBS - 1).astype(jnp.int32)
    vis_mask = draw_vis_mask(jax.random.fold_in(key_list[10], 71), 0)
    vis_source = draw_vis_source(jax.random.fold_in(key_list[10], 71), 0)
    return {"facet_temp": facet_temp, "emissivity": emissivity, "longwave_in": longwave_in, "albedo": albedo, "shortwave_in": shortwave_in, "dir_share": dir_share, "view_blocks": view_blocks, "vis_list": vis_list, "vis_mask": vis_mask, "vis_source": vis_source}


DIR_WEIGHTS = (0.06, 0.06, 0.22, 0.22, 0.22, 0.22)
SHORT_FACTOR = 0.7 / 0.97


def entry_slots(flat_mask, flat_source, tracer_count):
    tracer_ids = jnp.arange(tracer_count, dtype=jnp.int32)
    matching = (flat_source[:, None] == tracer_ids[None, :]).astype(jnp.int32)
    counted = matching * flat_mask[:, None]
    earlier = jnp.cumsum(counted, axis=0) - counted
    return jnp.sum(earlier * matching, axis=1).astype(jnp.int32)


def reference(facet_temp, emissivity, longwave_in, albedo, shortwave_in, dir_share, view_blocks, vis_list, vis_mask, vis_source):
    long_rad = emissivity[None] * facet_temp ** 4 + (1.0 - emissivity[None]) * longwave_in
    short_rad = albedo[None] * shortwave_in
    radiosity = jnp.stack([long_rad, short_rad], 0).astype(jnp.bfloat16)
    weighted = (dir_share.astype(jnp.float32)[:, None, None] * radiosity.astype(jnp.float32)[None]).astype(jnp.bfloat16)
    columns = DIRS * BANDS * HOURS
    weighted = weighted.reshape(columns, STRIPS, NBS, FR)
    owners = N_BLK * N_TILE
    mask_all = vis_mask.reshape(owners, TPD * K)
    source_all = vis_source.reshape(owners, TPD * K)
    list_all = vis_list.reshape(owners, TPD * K)

    def one_owner(owner_index):
        blk_index = owner_index // N_TILE
        tile_index = owner_index % N_TILE
        flat_mask = mask_all[owner_index]
        flat_source = source_all[owner_index]
        flat_ids = list_all[owner_index]
        position = jnp.minimum(entry_slots(flat_mask, flat_source, N_TILE), CAP - 1)
        owner_views = view_blocks[blk_index, :, tile_index].reshape(N_TILE * CAP, FR, TR)
        blocks = owner_views[flat_source * CAP + position] * flat_mask.astype(jnp.bfloat16)[:, None, None]
        strip_rows = weighted[:, tile_index]
        facet_rows = jnp.take(strip_rows, flat_ids, axis=1).reshape(columns, TPD, K * FR)
        blocks = blocks.reshape(TPD, K * FR, TR)
        return jnp.einsum("ctf,tfp->ctp", facet_rows.astype(jnp.float32), blocks.astype(jnp.float32))

    per_owner = lax.map(one_owner, jnp.arange(owners, dtype=jnp.int32))
    directional_flux = jnp.transpose(per_owner, (1, 0, 2, 3)).reshape(DIRS, BANDS, HOURS, owners * TPD * TR)
    weights = jnp.array(DIR_WEIGHTS, jnp.float32)[:, None, None]
    weighted_sum = jnp.sum(weights * (directional_flux[:, 0] + SHORT_FACTOR * directional_flux[:, 1]), axis=0)
    radiant_temp = weighted_sum ** 0.25
    return directional_flux, radiant_temp
```

```python
import functools

import jax
import jax.numpy as jnp
from jax import lax
from jax.experimental import pallas as pl
from jax.experimental.pallas import tpu as pltpu
from jax.sharding import PartitionSpec as P

DIRS = 6
BANDS = 2
HOURS = 48
NY = 4
NZ = 8
NT = NY * NZ
NB = 8
CUT = 4
DIR_WEIGHTS = (0.06, 0.06, 0.22, 0.22, 0.22, 0.22)
SHORT_FACTOR = 0.7 / 0.97
MESH = pl.DeviceIdType.MESH
RAD_ROWS = 112
STEP_SENDS = 6
UNROLL = 4
NEAR_AFTER = 1


def entry_slots(flat_mask, flat_source, tracer_count):
    tracer_ids = jnp.arange(tracer_count, dtype=jnp.int32)
    matching = (flat_source[:, None] == tracer_ids[None, :]).astype(jnp.int32)
    counted = matching * flat_mask[:, None]
    earlier = jnp.cumsum(counted, axis=0) - counted
    return jnp.sum(earlier * matching, axis=1)


def general(
    facet_temp,
    emissivity,
    longwave_in,
    albedo,
    shortwave_in,
    dir_share,
    view_blocks,
    vis_list,
    vis_mask,
    vis_source,
):
    long_rad = emissivity[None] * facet_temp**4 + (1.0 - emissivity[None]) * longwave_in
    short_rad = albedo[None] * shortwave_in
    radiosity = jnp.stack([long_rad, short_rad], 0).astype(jnp.bfloat16)
    local = jnp.concatenate(
        [radiosity.reshape(BANDS * HOURS, -1), dir_share.reshape(DIRS, -1)], axis=0
    )
    copies = jnp.broadcast_to(local[None], (lax.axis_size("blk"),) + local.shape)
    strip = lax.all_to_all(copies, "blk", split_axis=0, concat_axis=0, tiled=True)
    strip = jnp.transpose(strip, (1, 0, 2)).reshape(local.shape[0], -1).astype(jnp.float32)
    product = strip[BANDS * HOURS :, None, :] * strip[None, : BANDS * HOURS]
    strip_rows = product.astype(jnp.bfloat16).reshape(DIRS * BANDS * HOURS, -1)
    tracer_count = lax.axis_size("tile")
    capacity = view_blocks.shape[3]
    block_facets = view_blocks.shape[4]
    tile_points = view_blocks.shape[5]
    outgoing = view_blocks.reshape(tracer_count, capacity, block_facets, tile_points)
    received = lax.all_to_all(outgoing, "tile", split_axis=0, concat_axis=0, tiled=True)
    tiles_here, slot_count = vis_list.shape
    flat_mask = vis_mask.reshape(-1)
    flat_source = vis_source.reshape(-1)
    position = jnp.minimum(entry_slots(flat_mask, flat_source, tracer_count), capacity - 1)
    pick_index = flat_source * capacity + position
    blocks = received.reshape(tracer_count * capacity, block_facets, tile_points)[pick_index]
    blocks = blocks * flat_mask.astype(jnp.bfloat16)[:, None, None]
    blocks = blocks.reshape(tiles_here, slot_count * block_facets, tile_points)
    columns = strip_rows.shape[0]
    strip_blocks = strip_rows.reshape(columns, -1, block_facets)

    def one_tile(tile_args):
        tile_ids, tile_blocks = tile_args
        facet_rows = jnp.take(strip_blocks, tile_ids, axis=1).reshape(
            columns, slot_count * block_facets
        )
        return jnp.dot(facet_rows, tile_blocks, preferred_element_type=jnp.float32)

    per_tile = lax.map(one_tile, (vis_list, blocks))
    flux = jnp.transpose(per_tile, (1, 0, 2)).reshape(columns, tiles_here * tile_points)
    directional = flux.reshape(DIRS, BANDS, HOURS, -1)
    weights = jnp.array(DIR_WEIGHTS, jnp.float32)[:, None, None]
    weighted_sum = jnp.sum(
        weights * (directional[:, 0] + SHORT_FACTOR * directional[:, 1]), axis=0
    )
    return flux, weighted_sum**0.25


def within(index, size):
    return jnp.minimum(jnp.maximum(index, 0), size - 1)


def column_of(x):
    rows, width = x.shape
    eye = lax.broadcasted_iota(jnp.int32, (width, width), 0) == lax.broadcasted_iota(
        jnp.int32, (width, width), 1
    )
    parts = []
    for i in range(rows):
        line = jnp.broadcast_to(x[i : i + 1, :].astype(jnp.float32), (width, width))
        parts.append(jnp.sum(jnp.where(eye, line, 0.0), axis=1, keepdims=True))
    return jnp.concatenate(parts, axis=0)


def fill_flag(mask_ref, source_ref, flag):
    mask = column_of(mask_ref[...])
    source = column_of(source_ref[...])
    lane = lax.broadcasted_iota(jnp.int32, (mask.shape[0], 128), 1).astype(jnp.float32)
    named = jnp.sum(jnp.where((mask > 0.5) & (source == lane), 1.0, 0.0), axis=0, keepdims=True)
    most = jnp.max(named, axis=1, keepdims=True)
    flag[...] = jnp.broadcast_to(jnp.where(most > CUT + 0.5, 1, 0), flag.shape).astype(jnp.int32)


def fill_tables(list_ref, mask_ref, source_ref, table, ends):
    entries = mask_ref.shape[0] * mask_ref.shape[1]
    slots = mask_ref.shape[1]
    ids = column_of(list_ref[...])
    mask = column_of(mask_ref[...])
    source = column_of(source_ref[...])
    used = mask > 0.5
    entry = lax.broadcasted_iota(jnp.int32, (entries, 1), 0)
    tile = (entry // slots).astype(jnp.float32)
    before = (
        lax.broadcasted_iota(jnp.int32, (entries, entries), 1)
        < lax.broadcasted_iota(jnp.int32, (entries, entries), 0)
    ).astype(jnp.bfloat16)
    lane = lax.broadcasted_iota(jnp.int32, (entries, 128), 1).astype(jnp.float32)

    def earlier(chosen):
        count = jnp.dot(before, chosen.astype(jnp.bfloat16), preferred_element_type=jnp.float32)
        return jnp.sum(count * chosen, axis=1, keepdims=True)

    by_source = jnp.where(used & (source == lane), 1.0, 0.0)
    position = earlier(by_source)
    by_position = jnp.where(used & (position == lane), 1.0, 0.0)
    rank = earlier(by_position)
    place = position * NT + rank
    wide = lax.broadcasted_iota(jnp.int32, (entries, entries), 1).astype(jnp.float32)
    at = jnp.where(used & (place == wide), 1.0, 0.0)
    table[...] = jnp.zeros_like(table)
    table[0:1, :] = jnp.sum(at * ids, axis=0, keepdims=True).astype(jnp.int32)
    table[1:2, :] = jnp.sum(at * source, axis=0, keepdims=True).astype(jnp.int32)
    table[2:3, :] = jnp.sum(at * tile, axis=0, keepdims=True).astype(jnp.int32)
    up_to = jnp.where(tile <= lane, 1.0, 0.0)
    for p in range(8):
        chosen = jnp.sum(jnp.where(lane == float(p), by_position, 0.0), axis=1, keepdims=True)
        ends[p : p + 1, :] = jnp.sum(chosen * up_to, axis=0, keepdims=True).astype(jnp.int32)


def kernel(
    view, temp_in, emis, longwave, albedo, short, share, list_ref, mask_ref, source_ref,
    flux, radiant, bad,
    low0, low1, low2, low3, high, near, rad, rows, running, table, ends, flag, flags, pick, over, overs,
    table_s, ends_s, pick_s,
    low_send, low_recv, ring_send, ring_recv, col_send, col_recv, rad_send, rad_recv,
    flag_send, flag_recv, over_send, over_recv, local,
):
    b = lax.axis_index("blk")
    t = lax.axis_index("tile")
    y = t // NZ
    z = lax.rem(t, NZ)

    def tile_peer(i):
        return lax.rem(y + i // NZ, NY) * NZ + lax.rem(z + lax.rem(i, NZ), NZ)

    barrier = pltpu.get_barrier_semaphore()

    def greet_tile(i, carry):
        pl.semaphore_signal(
            barrier, inc=1, device_id=(b, lax.rem(t + i, NT)), device_id_type=MESH
        )
        return carry

    def greet_blk(i, carry):
        pl.semaphore_signal(
            barrier, inc=1, device_id=(lax.rem(b + i, NB), t), device_id_type=MESH
        )
        return carry

    lax.fori_loop(1, NT, greet_tile, 0)
    lax.fori_loop(1, NB, greet_blk, 0)

    high_copy = pltpu.make_async_copy(view.at[:, pl.ds(CUT, CUT)], high, local.at[0])
    high_copy.start()
    low = (low0, low1, low2, low3)
    own_copies = [
        pltpu.make_async_copy(view.at[t, p], low[p].at[t], local.at[5 + p]) for p in range(CUT)
    ]
    for copy in own_copies:
        copy.start()

    emissivity = emis[...]
    long_rad = emissivity * temp_in[:, 0, :] ** 4 + (1.0 - emissivity) * longwave[:, 0, :]
    rad[b, 0:HOURS, :] = long_rad.astype(jnp.bfloat16)
    rad[b, HOURS : 2 * HOURS, :] = (albedo[...] * short[:, 0, :]).astype(jnp.bfloat16)
    rad[b, 2 * HOURS : RAD_ROWS, :] = jnp.concatenate(
        [share[...].astype(jnp.float32), jnp.zeros((RAD_ROWS - 2 * HOURS - DIRS, share.shape[1]), jnp.float32)],
        axis=0,
    ).astype(jnp.bfloat16)
    fill_flag(mask_ref, source_ref, flag)
    flags[t] = flag[...]
    running[0] = jnp.zeros(running.shape[1:], jnp.float32)

    pl.semaphore_wait(barrier, NT - 1 + NB - 1)

    def flag_to(i):
        return pltpu.make_async_remote_copy(
            src_ref=flag, dst_ref=flags.at[t], send_sem=flag_send.at[i], recv_sem=flag_recv.at[i],
            device_id=(b, tile_peer(i)), device_id_type=MESH,
        )

    def rad_to(i):
        return pltpu.make_async_remote_copy(
            src_ref=rad.at[b], dst_ref=rad.at[b], send_sem=rad_send.at[i], recv_sem=rad_recv.at[i],
            device_id=(lax.rem(b + i, NB), t), device_id_type=MESH,
        )

    def low_to(p, i):
        return pltpu.make_async_remote_copy(
            src_ref=view.at[tile_peer(i), p], dst_ref=low[p].at[t],
            send_sem=low_send.at[p, i], recv_sem=low_recv.at[p, i],
            device_id=(b, tile_peer(i)), device_id_type=MESH,
        )

    def over_to(i):
        return pltpu.make_async_remote_copy(
            src_ref=over, dst_ref=overs.at[b], send_sem=over_send.at[i], recv_sem=over_recv.at[i],
            device_id=(lax.rem(b + i, NB), t), device_id_type=MESH,
        )

    def ring_to(way, step):
        toward = lax.rem(z + (1, NZ - 1)[way], NZ)
        behind = y * NZ + lax.rem(z + (NZ - step, step)[way], NZ)
        half = CUT // 2
        part = pl.ds(0, CUT) if step < NZ // 2 - 1 else pl.ds(way * half, half)
        return pltpu.make_async_remote_copy(
            src_ref=near.at[behind, part], dst_ref=near.at[behind, part],
            send_sem=ring_send.at[way, step], recv_sem=ring_recv.at[way, step],
            device_id=(b, y * NZ + toward), device_id_type=MESH,
        )

    def column_to(dy, dz):
        held = y * NZ + lax.rem(z + dz, NZ)
        return pltpu.make_async_remote_copy(
            src_ref=near.at[held], dst_ref=near.at[held],
            send_sem=col_send.at[dy, dz], recv_sem=col_recv.at[dy, dz],
            device_id=(b, lax.rem(y + dy, NY) * NZ + z), device_id_type=MESH,
        )

    def looped(lo, hi, action):
        def body(i, carry):
            action(i)
            return carry

        lax.fori_loop(lo, hi, body, 0)

    sent = [1]

    def send_low(count):
        k = sent[0]
        end = min(CUT * NT, k + count)
        while k < end:
            p = k // NT
            stop = min(end, (p + 1) * NT)
            looped(max(k - p * NT, 1), stop - p * NT, lambda i: low_to(p, i).start())
            k = stop
        sent[0] = k

    looped(1, NT, lambda i: flag_to(i).start())
    send_low(STEP_SENDS)
    looped(1, NB, lambda i: rad_to(i).start())
    looped(1, NT, lambda i: flag_to(i).wait())
    total = jnp.zeros((8, 128), jnp.int32)
    where_to = jnp.zeros((8, 128), jnp.int32)
    for o in range(NT):
        total += flags[o]
        where_to += flags[o] * o
    pick[...] = jnp.where(total == 1, where_to, 0)
    over[...] = jnp.where(total > 1, 1, 0).astype(jnp.int32)
    overs[b] = over[...]
    pick_copy = pltpu.make_async_copy(pick, pick_s, local.at[4])
    pick_copy.start()
    looped(1, NB, lambda i: over_to(i).start())
    high_copy.wait()
    pick_copy.wait()
    near[t] = high[within(pick_s[0, 0], NT)]

    for step in range(NZ // 2):
        ring_to(0, step).start()
        ring_to(1, step).start()
        if step == 0:
            shares = [0]
        else:
            shares = [step, NZ - step]
        for dz in shares:
            for dy in range(1, NY):
                column_to(dy, dz).start()
        send_low(STEP_SENDS)
        ring_to(0, step).wait()
        ring_to(1, step).wait()
    for dy in range(1, NY):
        column_to(dy, NZ // 2).start()
    send_low(CUT * NT)

    fill_tables(list_ref, mask_ref, source_ref, table, ends)
    table_copy = pltpu.make_async_copy(table, table_s, local.at[2])
    table_copy.start()
    ends_copy = pltpu.make_async_copy(ends, ends_s, local.at[3])
    ends_copy.start()
    for copy in own_copies:
        copy.wait()
    table_copy.wait()
    ends_copy.wait()
    looped(1, NB, lambda i: rad_to(i).wait())

    facet_blocks = rad.shape[2] // 128

    def weight(j, carry):
        for q in range(facet_blocks):
            cols = slice(q * 128, (q + 1) * 128)
            radiosity = rad[j, 0 : 2 * HOURS, cols].astype(jnp.float32)
            shares = rad[j, 2 * HOURS : RAD_ROWS, cols].astype(jnp.float32)
            for d in range(DIRS):
                rows[j * facet_blocks + q, d * 2 * HOURS : (d + 1) * 2 * HOURS, :] = (
                    shares[d : d + 1, :] * radiosity
                ).astype(jnp.bfloat16)
        return carry

    lax.fori_loop(0, NB, weight, 0)

    tiles = mask_ref.shape[0]

    def position_products(p, held, first_phase):
        def body(turn, carry):
            for u in range(UNROLL):
                r = turn * UNROLL + u
                g = p * NT + r
                same = (r > 0) & (table_s[2, g] == table_s[2, jnp.maximum(g - 1, 0)])
                product = jnp.dot(
                    rows[within(table_s[0, g], rows.shape[0])],
                    held(within(table_s[1, g], NT)),
                    preferred_element_type=jnp.float32,
                )
                running[r + 1] = product + jnp.where(same, running[r], 0.0)
            return carry

        lax.fori_loop(0, NT // UNROLL, body, 0)
        for i in range(tiles):
            end = within(ends_s[p, i], NT + 1)
            start = within(ends_s[p, i - 1], NT + 1) if i else 0
            cols = slice(i * 128, (i + 1) * 128)
            part = jnp.where(end > start, running[end], 0.0)
            if first_phase:
                flux[:, cols] = part
            else:
                flux[:, cols] += part

    def low_wait(p):
        looped(1, NT, lambda i: low_to(p, i).wait())

    looped(1, NB, lambda i: over_to(i).wait())
    any_over = overs[0]
    for i in range(1, NB):
        any_over += overs[i]
    over[...] = any_over
    over_copy = pltpu.make_async_copy(over, pick_s, local.at[4])
    over_copy.start()
    over_copy.wait()
    bad[0, 0] = pick_s[0, 0]

    for p in range(CUT):
        low_wait(p)
        position_products(p, lambda s: low[p][s], p == 0)
        if p == NEAR_AFTER:
            for dy in range(1, NY):
                looped(0, NZ, lambda dz: column_to(dy, dz).wait())
            for q in range(CUT):
                position_products(CUT + q, lambda s: near[s, q], False)

    total_flux = jnp.zeros((HOURS, flux.shape[1]), jnp.float32)
    for d in range(DIRS):
        base = d * 2 * HOURS
        total_flux += DIR_WEIGHTS[d] * (
            flux[base : base + HOURS, :] + SHORT_FACTOR * flux[base + HOURS : base + 2 * HOURS, :]
        )
    radiant[...] = jnp.sqrt(jnp.sqrt(total_flux))


def shards(*args):
    (facet_temp, emissivity, longwave_in, albedo, shortwave_in, dir_share, view_blocks,
     vis_list, vis_mask, vis_source) = args
    width = facet_temp.shape[2]
    capacity, facets, points = view_blocks.shape[3:]
    tiles, slots = vis_list.shape
    columns = DIRS * BANDS * HOURS
    assert capacity == 2 * CUT and tiles * slots == capacity * NT
    view = view_blocks.reshape(NT, capacity, facets, points)
    vmem = pl.BlockSpec(memory_space=pltpu.VMEM)
    dma = pltpu.SemaphoreType.DMA
    flux, radiant, bad = pl.pallas_call(
        kernel,
        out_shape=(
            jax.ShapeDtypeStruct((columns, tiles * points), jnp.float32),
            jax.ShapeDtypeStruct((HOURS, tiles * points), jnp.float32),
            jax.ShapeDtypeStruct((1, 1), jnp.int32),
        ),
        in_specs=[pl.BlockSpec(memory_space=pl.ANY)] + [vmem] * 9,
        out_specs=(vmem, vmem, pl.BlockSpec(memory_space=pltpu.SMEM)),
        scratch_shapes=[
            *([pltpu.VMEM((NT, facets, points), jnp.bfloat16)] * CUT),
            pltpu.VMEM((NT, CUT, facets, points), jnp.bfloat16),
            pltpu.VMEM((NT, CUT, facets, points), jnp.bfloat16),
            pltpu.VMEM((NB, RAD_ROWS, width), jnp.bfloat16),
            pltpu.VMEM((NB * width // facets, columns, facets), jnp.bfloat16),
            pltpu.VMEM((NT + 1, columns, points), jnp.float32),
            pltpu.VMEM((8, tiles * slots), jnp.int32),
            pltpu.VMEM((8, 128), jnp.int32),
            pltpu.VMEM((8, 128), jnp.int32),
            pltpu.VMEM((NT, 8, 128), jnp.int32),
            pltpu.VMEM((8, 128), jnp.int32),
            pltpu.VMEM((8, 128), jnp.int32),
            pltpu.VMEM((NB, 8, 128), jnp.int32),
            pltpu.SMEM((8, tiles * slots), jnp.int32),
            pltpu.SMEM((8, 128), jnp.int32),
            pltpu.SMEM((8, 128), jnp.int32),
            dma((CUT, NT)),
            dma((CUT, NT)),
            dma((2, NZ // 2)),
            dma((2, NZ // 2)),
            dma((NY, NZ)),
            dma((NY, NZ)),
            dma((NB,)),
            dma((NB,)),
            dma((NT,)),
            dma((NT,)),
            dma((NB,)),
            dma((NB,)),
            dma((5 + CUT,)),
        ],
        compiler_params=pltpu.CompilerParams(
            collective_id=0, has_side_effects=True, vmem_limit_bytes=38 * 1024 * 1024
        ),
    )(
        view,
        facet_temp,
        emissivity,
        longwave_in,
        albedo,
        shortwave_in,
        dir_share.reshape(DIRS, width),
        vis_list,
        vis_mask,
        vis_source,
    )
    flux, radiant = lax.cond(
        bad[0, 0] > 0, lambda: general(*args), lambda: (flux, radiant)
    )
    return flux.reshape(DIRS, BANDS, HOURS, tiles * points), radiant


def solution(mesh):
    in_specs = (
        P(None, "tile", "blk"),
        P("tile", "blk"),
        P(None, "tile", "blk"),
        P("tile", "blk"),
        P(None, "tile", "blk"),
        P(None, "tile", "blk"),
        P("blk", "tile", None, None, None, None),
        P(("blk", "tile"), None),
        P(("blk", "tile"), None),
        P(("blk", "tile"), None),
    )
    out_specs = (P(None, None, None, ("blk", "tile")), P(None, ("blk", "tile")))
    return jax.shard_map(shards, mesh=mesh, in_specs=in_specs, out_specs=out_specs, check_vma=False)
```

```python
import functools

import jax
import jax.numpy as jnp
from jax import lax
from jax.experimental import pallas as pl
from jax.experimental.pallas import tpu as pltpu
from jax.sharding import PartitionSpec as P

DIRS = 6
BANDS = 2
HOURS = 48
NY = 4
NZ = 8
NT = NY * NZ
NB = 8
CUT = 4
DIR_WEIGHTS = (0.06, 0.06, 0.22, 0.22, 0.22, 0.22)
SHORT_FACTOR = 0.7 / 0.97
MESH = pl.DeviceIdType.MESH
RAD_ROWS = 112
FIRST_SENDS = 12
LOW_PER_COLUMN = 2
UNROLL = 8
NEAR_AFTER = 1


def entry_slots(flat_mask, flat_source, tracer_count):
    tracer_ids = jnp.arange(tracer_count, dtype=jnp.int32)
    matching = (flat_source[:, None] == tracer_ids[None, :]).astype(jnp.int32)
    counted = matching * flat_mask[:, None]
    earlier = jnp.cumsum(counted, axis=0) - counted
    return jnp.sum(earlier * matching, axis=1)


def general(
    facet_temp,
    emissivity,
    longwave_in,
    albedo,
    shortwave_in,
    dir_share,
    view_blocks,
    vis_list,
    vis_mask,
    vis_source,
):
    long_rad = emissivity[None] * facet_temp**4 + (1.0 - emissivity[None]) * longwave_in
    short_rad = albedo[None] * shortwave_in
    radiosity = jnp.stack([long_rad, short_rad], 0).astype(jnp.bfloat16)
    local = jnp.concatenate(
        [radiosity.reshape(BANDS * HOURS, -1), dir_share.reshape(DIRS, -1)], axis=0
    )
    copies = jnp.broadcast_to(local[None], (lax.axis_size("blk"),) + local.shape)
    strip = lax.all_to_all(copies, "blk", split_axis=0, concat_axis=0, tiled=True)
    strip = jnp.transpose(strip, (1, 0, 2)).reshape(local.shape[0], -1).astype(jnp.float32)
    product = strip[BANDS * HOURS :, None, :] * strip[None, : BANDS * HOURS]
    strip_rows = product.astype(jnp.bfloat16).reshape(DIRS * BANDS * HOURS, -1)
    tracer_count = lax.axis_size("tile")
    capacity = view_blocks.shape[3]
    block_facets = view_blocks.shape[4]
    tile_points = view_blocks.shape[5]
    outgoing = view_blocks.reshape(tracer_count, capacity, block_facets, tile_points)
    received = lax.all_to_all(outgoing, "tile", split_axis=0, concat_axis=0, tiled=True)
    tiles_here, slot_count = vis_list.shape
    flat_mask = vis_mask.reshape(-1)
    flat_source = vis_source.reshape(-1)
    position = jnp.minimum(entry_slots(flat_mask, flat_source, tracer_count), capacity - 1)
    pick_index = flat_source * capacity + position
    blocks = received.reshape(tracer_count * capacity, block_facets, tile_points)[pick_index]
    blocks = blocks * flat_mask.astype(jnp.bfloat16)[:, None, None]
    blocks = blocks.reshape(tiles_here, slot_count * block_facets, tile_points)
    columns = strip_rows.shape[0]
    strip_blocks = strip_rows.reshape(columns, -1, block_facets)

    def one_tile(tile_args):
        tile_ids, tile_blocks = tile_args
        facet_rows = jnp.take(strip_blocks, tile_ids, axis=1).reshape(
            columns, slot_count * block_facets
        )
        return jnp.dot(facet_rows, tile_blocks, preferred_element_type=jnp.float32)

    per_tile = lax.map(one_tile, (vis_list, blocks))
    flux = jnp.transpose(per_tile, (1, 0, 2)).reshape(columns, tiles_here * tile_points)
    return flux


def within(index, size):
    return jnp.minimum(jnp.maximum(index, 0), size - 1)


def column_of(x):
    rows, width = x.shape
    eye = lax.broadcasted_iota(jnp.int32, (width, width), 0) == lax.broadcasted_iota(
        jnp.int32, (width, width), 1
    )
    parts = []
    for i in range(rows):
        line = jnp.broadcast_to(x[i : i + 1, :].astype(jnp.float32), (width, width))
        parts.append(jnp.sum(jnp.where(eye, line, 0.0), axis=1, keepdims=True))
    return jnp.concatenate(parts, axis=0)


def fill_flag(mask_ref, source_ref, flag):
    mask = column_of(mask_ref[...])
    source = column_of(source_ref[...])
    lane = lax.broadcasted_iota(jnp.int32, (mask.shape[0], 128), 1).astype(jnp.float32)
    named = jnp.sum(jnp.where((mask > 0.5) & (source == lane), 1.0, 0.0), axis=0, keepdims=True)
    most = jnp.max(named, axis=1, keepdims=True)
    flag[...] = jnp.broadcast_to(jnp.where(most > CUT + 0.5, 1, 0), flag.shape).astype(jnp.int32)


def fill_tables(list_ref, mask_ref, source_ref, table, ends):
    entries = mask_ref.shape[0] * mask_ref.shape[1]
    slots = mask_ref.shape[1]
    ids = column_of(list_ref[...])
    mask = column_of(mask_ref[...])
    source = column_of(source_ref[...])
    used = mask > 0.5
    entry = lax.broadcasted_iota(jnp.int32, (entries, 1), 0)
    tile = (entry // slots).astype(jnp.float32)
    before = (
        lax.broadcasted_iota(jnp.int32, (entries, entries), 1)
        < lax.broadcasted_iota(jnp.int32, (entries, entries), 0)
    ).astype(jnp.bfloat16)
    lane = lax.broadcasted_iota(jnp.int32, (entries, 128), 1).astype(jnp.float32)

    def earlier(chosen):
        count = jnp.dot(before, chosen.astype(jnp.bfloat16), preferred_element_type=jnp.float32)
        return jnp.sum(count * chosen, axis=1, keepdims=True)

    by_source = jnp.where(used & (source == lane), 1.0, 0.0)
    position = earlier(by_source)
    by_position = jnp.where(used & (position == lane), 1.0, 0.0)
    rank = earlier(by_position)
    place = position * NT + rank
    wide = lax.broadcasted_iota(jnp.int32, (entries, entries), 1).astype(jnp.float32)
    at = jnp.where(used & (place == wide), 1.0, 0.0)
    table[...] = jnp.zeros_like(table)
    table[0:1, :] = jnp.sum(at * ids, axis=0, keepdims=True).astype(jnp.int32)
    table[1:2, :] = jnp.sum(at * source, axis=0, keepdims=True).astype(jnp.int32)
    table[2:3, :] = jnp.sum(at * tile, axis=0, keepdims=True).astype(jnp.int32)
    up_to = jnp.where(tile <= lane, 1.0, 0.0)
    for p in range(8):
        chosen = jnp.sum(jnp.where(lane == float(p), by_position, 0.0), axis=1, keepdims=True)
        ends[p : p + 1, :] = jnp.sum(chosen * up_to, axis=0, keepdims=True).astype(jnp.int32)


def kernel(
    view, temp_in, emis, longwave, albedo, short, share, list_ref, mask_ref, source_ref,
    flux, bad,
    low0, low1, low2, low3, high, near, rad, rows, running, table, ends, flag, flags, sums, pick, over, overs,
    table_s, ends_s, pick_s,
    low_send, low_recv, ring_send, ring_recv, col_send, col_recv, rad_send, rad_recv,
    flag_send, flag_recv, over_send, over_recv, local, row_here,
):
    b = lax.axis_index("blk")
    t = lax.axis_index("tile")
    y = t // NZ
    z = lax.rem(t, NZ)

    def tile_peer(i):
        return lax.rem(y + i // NZ, NY) * NZ + lax.rem(z + lax.rem(i, NZ), NZ)

    barrier = pltpu.get_barrier_semaphore()

    for i in range(1, NZ):
        pl.semaphore_signal(barrier, inc=1, device_id=(b, tile_peer(i)), device_id_type=MESH)
    for i in range(NZ, NT, NZ):
        pl.semaphore_signal(barrier, inc=1, device_id=(b, tile_peer(i)), device_id_type=MESH)
    for i in range(1, NB):
        pl.semaphore_signal(
            barrier, inc=1, device_id=(lax.rem(b + i, NB), t), device_id_type=MESH
        )

    high_copy = pltpu.make_async_copy(view.at[:, pl.ds(CUT, CUT)], high, local.at[0])
    high_copy.start()
    low = (low0, low1, low2, low3)
    own_copies = [
        pltpu.make_async_copy(view.at[t, p], low[p].at[t], local.at[5 + p]) for p in range(CUT)
    ]
    for copy in own_copies:
        copy.start()

    emissivity = emis[...]
    long_rad = emissivity * temp_in[:, 0, :] ** 4 + (1.0 - emissivity) * longwave[:, 0, :]
    rad[b, 0:HOURS, :] = long_rad.astype(jnp.bfloat16)
    rad[b, HOURS : 2 * HOURS, :] = (albedo[...] * short[:, 0, :]).astype(jnp.bfloat16)
    rad[b, 2 * HOURS : RAD_ROWS, :] = jnp.concatenate(
        [share[...].astype(jnp.float32), jnp.zeros((RAD_ROWS - 2 * HOURS - DIRS, share.shape[1]), jnp.float32)],
        axis=0,
    ).astype(jnp.bfloat16)
    fill_flag(mask_ref, source_ref, flag)
    flags[z] = flag[...]
    running[0] = jnp.zeros(running.shape[1:], jnp.float32)

    pl.semaphore_wait(barrier, NZ - 1 + NY - 1 + NB - 1)
    for i in range(NZ, NT, NZ):
        pl.semaphore_signal(row_here, inc=1, device_id=(b, tile_peer(i)), device_id_type=MESH)

    def flag_to(i):
        return pltpu.make_async_remote_copy(
            src_ref=flag, dst_ref=flags.at[z], send_sem=flag_send.at[i], recv_sem=flag_recv.at[i],
            device_id=(b, tile_peer(i)), device_id_type=MESH,
        )

    def sums_to(i):
        return pltpu.make_async_remote_copy(
            src_ref=sums.at[y], dst_ref=sums.at[y],
            send_sem=flag_send.at[NZ + i], recv_sem=flag_recv.at[NZ + i],
            device_id=(b, tile_peer(i * NZ)), device_id_type=MESH,
        )

    def rad_to(i):
        return pltpu.make_async_remote_copy(
            src_ref=rad.at[b], dst_ref=rad.at[b], send_sem=rad_send.at[i], recv_sem=rad_recv.at[i],
            device_id=(lax.rem(b + i, NB), t), device_id_type=MESH,
        )

    def low_to(p, i):
        return pltpu.make_async_remote_copy(
            src_ref=view.at[tile_peer(i), p], dst_ref=low[p].at[t],
            send_sem=low_send.at[p, i], recv_sem=low_recv.at[p, i],
            device_id=(b, tile_peer(i)), device_id_type=MESH,
        )

    def over_to(i):
        return pltpu.make_async_remote_copy(
            src_ref=over, dst_ref=overs.at[b], send_sem=over_send.at[i], recv_sem=over_recv.at[i],
            device_id=(lax.rem(b + i, NB), t), device_id_type=MESH,
        )

    def ring_to(way, step):
        toward = lax.rem(z + (1, NZ - 1)[way], NZ)
        behind = y * NZ + lax.rem(z + (NZ - step, step)[way], NZ)
        half = CUT // 2
        part = pl.ds(0, CUT) if step < NZ // 2 - 1 else pl.ds(way * half, half)
        return pltpu.make_async_remote_copy(
            src_ref=near.at[behind, part], dst_ref=near.at[behind, part],
            send_sem=ring_send.at[way, step], recv_sem=ring_recv.at[way, step],
            device_id=(b, y * NZ + toward), device_id_type=MESH,
        )

    def column_to(dy, dz):
        held = y * NZ + lax.rem(z + dz, NZ)
        return pltpu.make_async_remote_copy(
            src_ref=near.at[held], dst_ref=near.at[held],
            send_sem=col_send.at[dy, dz], recv_sem=col_recv.at[dy, dz],
            device_id=(b, lax.rem(y + dy, NY) * NZ + z), device_id_type=MESH,
        )

    def looped(lo, hi, action):
        def body(i, carry):
            action(i)
            return carry

        lax.fori_loop(lo, hi, body, 0)

    sent = [1]

    def send_low(count):
        k = sent[0]
        end = min(CUT * NT, k + count)
        while k < end:
            p = k // NT
            stop = min(end, (p + 1) * NT)
            looped(max(k - p * NT, 1), stop - p * NT, lambda i: low_to(p, i).start())
            k = stop
        sent[0] = k

    for i in range(1, NZ):
        flag_to(i).start()
    send_low(NZ - 1)
    pl.semaphore_wait(row_here, NY - 1)
    send_low(FIRST_SENDS // 2)
    for i in range(1, NZ):
        flag_to(i).wait()
    total = jnp.zeros((8, 128), jnp.int32)
    where_to = jnp.zeros((8, 128), jnp.int32)
    for o in range(NZ):
        total += flags[o]
        where_to += flags[o] * (y * NZ + o)
    sums[y, 0] = total
    sums[y, 1] = where_to
    for i in range(1, NY):
        sums_to(i).start()
    send_low(FIRST_SENDS // 2)
    looped(1, NB, lambda i: rad_to(i).start())
    for i in range(1, NY):
        sums_to(i).wait()
    total = sums[0, 0]
    where_to = sums[0, 1]
    for i in range(1, NY):
        total += sums[i, 0]
        where_to += sums[i, 1]
    pick[...] = jnp.where(total == 1, where_to, 0)
    over[...] = jnp.where(total > 1, 1, 0).astype(jnp.int32)
    overs[b] = over[...]
    pick_copy = pltpu.make_async_copy(pick, pick_s, local.at[4])
    pick_copy.start()
    looped(1, NB, lambda i: over_to(i).start())
    high_copy.wait()
    pick_copy.wait()
    near[t] = high[within(pick_s[0, 0], NT)]

    for step in range(NZ // 2):
        ring_to(0, step).start()
        ring_to(1, step).start()
        if step == 0:
            shares = [0]
        else:
            shares = [step, NZ - step]
        for dz in shares:
            for dy in range(1, NY):
                column_to(dy, dz).start()
                send_low(LOW_PER_COLUMN)
        ring_to(0, step).wait()
        ring_to(1, step).wait()
    for dy in range(1, NY):
        column_to(dy, NZ // 2).start()
        send_low(LOW_PER_COLUMN)
    send_low(CUT * NT)

    fill_tables(list_ref, mask_ref, source_ref, table, ends)
    table_copy = pltpu.make_async_copy(table, table_s, local.at[2])
    table_copy.start()
    ends_copy = pltpu.make_async_copy(ends, ends_s, local.at[3])
    ends_copy.start()
    for copy in own_copies:
        copy.wait()
    table_copy.wait()
    ends_copy.wait()
    looped(1, NB, lambda i: rad_to(i).wait())

    facet_blocks = rad.shape[2] // 128

    def weight(j, carry):
        for q in range(facet_blocks):
            cols = slice(q * 128, (q + 1) * 128)
            radiosity = rad[j, 0 : 2 * HOURS, cols].astype(jnp.float32)
            shares = rad[j, 2 * HOURS : RAD_ROWS, cols].astype(jnp.float32)
            for d in range(DIRS):
                rows[j * facet_blocks + q, d * 2 * HOURS : (d + 1) * 2 * HOURS, :] = (
                    shares[d : d + 1, :] * radiosity
                ).astype(jnp.bfloat16)
        return carry

    lax.fori_loop(0, NB, weight, 0)

    tiles = mask_ref.shape[0]

    def position_products(p, held, first_phase):
        def body(turn, carry):
            for u in range(UNROLL):
                r = turn * UNROLL + u
                g = p * NT + r
                same = (r > 0) & (table_s[2, g] == table_s[2, jnp.maximum(g - 1, 0)])
                product = jnp.dot(
                    rows[within(table_s[0, g], rows.shape[0])],
                    held(within(table_s[1, g], NT)),
                    preferred_element_type=jnp.float32,
                )
                running[r + 1] = product + jnp.where(same, running[r], 0.0)
            return carry

        lax.fori_loop(0, NT // UNROLL, body, 0)
        for i in range(tiles):
            end = within(ends_s[p, i], NT + 1)
            start = within(ends_s[p, i - 1], NT + 1) if i else 0
            cols = slice(i * 128, (i + 1) * 128)
            part = jnp.where(end > start, running[end], 0.0)
            if first_phase:
                flux[:, cols] = part
            else:
                flux[:, cols] += part

    def low_wait(p):
        looped(1, NT, lambda i: low_to(p, i).wait())

    looped(1, NB, lambda i: over_to(i).wait())
    any_over = overs[0]
    for i in range(1, NB):
        any_over += overs[i]
    over[...] = any_over
    over_copy = pltpu.make_async_copy(over, pick_s, local.at[4])
    over_copy.start()
    over_copy.wait()
    bad[0, 0] = pick_s[0, 0]

    for p in range(CUT):
        low_wait(p)
        position_products(p, lambda s: low[p][s], p == 0)
        if p == NEAR_AFTER:
            for dy in range(1, NY):
                looped(0, NZ, lambda dz: column_to(dy, dz).wait())
            for q in range(CUT):
                position_products(CUT + q, lambda s: near[s, q], False)


def finish(found, flux, radiant):
    total = None
    for d in range(DIRS):
        base = d * 2 * HOURS
        part = DIR_WEIGHTS[d] * (
            found[base : base + HOURS, :] + SHORT_FACTOR * found[base + HOURS : base + 2 * HOURS, :]
        )
        total = part if total is None else total + part
    radiant[...] = jnp.sqrt(jnp.sqrt(total))
    flux[...] = found[...]


def shards(*args):
    (facet_temp, emissivity, longwave_in, albedo, shortwave_in, dir_share, view_blocks,
     vis_list, vis_mask, vis_source) = args
    width = facet_temp.shape[2]
    capacity, facets, points = view_blocks.shape[3:]
    tiles, slots = vis_list.shape
    columns = DIRS * BANDS * HOURS
    assert capacity == 2 * CUT and tiles * slots == capacity * NT
    view = view_blocks.reshape(NT, capacity, facets, points)
    vmem = pl.BlockSpec(memory_space=pltpu.VMEM)
    dma = pltpu.SemaphoreType.DMA
    found, bad = pl.pallas_call(
        kernel,
        out_shape=(
            jax.ShapeDtypeStruct((columns, tiles * points), jnp.float32),
            jax.ShapeDtypeStruct((1, 1), jnp.int32),
        ),
        in_specs=[pl.BlockSpec(memory_space=pl.ANY)] + [vmem] * 9,
        out_specs=(vmem, pl.BlockSpec(memory_space=pltpu.SMEM)),
        scratch_shapes=[
            *([pltpu.VMEM((NT, facets, points), jnp.bfloat16)] * CUT),
            pltpu.VMEM((NT, CUT, facets, points), jnp.bfloat16),
            pltpu.VMEM((NT, CUT, facets, points), jnp.bfloat16),
            pltpu.VMEM((NB, RAD_ROWS, width), jnp.bfloat16),
            pltpu.VMEM((NB * width // facets, columns, facets), jnp.bfloat16),
            pltpu.VMEM((NT + 1, columns, points), jnp.float32),
            pltpu.VMEM((8, tiles * slots), jnp.int32),
            pltpu.VMEM((8, 128), jnp.int32),
            pltpu.VMEM((8, 128), jnp.int32),
            pltpu.VMEM((NZ, 8, 128), jnp.int32),
            pltpu.VMEM((NY, 2, 8, 128), jnp.int32),
            pltpu.VMEM((8, 128), jnp.int32),
            pltpu.VMEM((8, 128), jnp.int32),
            pltpu.VMEM((NB, 8, 128), jnp.int32),
            pltpu.SMEM((8, tiles * slots), jnp.int32),
            pltpu.SMEM((8, 128), jnp.int32),
            pltpu.SMEM((8, 128), jnp.int32),
            dma((CUT, NT)),
            dma((CUT, NT)),
            dma((2, NZ // 2)),
            dma((2, NZ // 2)),
            dma((NY, NZ)),
            dma((NY, NZ)),
            dma((NB,)),
            dma((NB,)),
            dma((NT,)),
            dma((NT,)),
            dma((NB,)),
            dma((NB,)),
            dma((5 + CUT,)),
            pltpu.SemaphoreType.REGULAR,
        ],
        compiler_params=pltpu.CompilerParams(
            collective_id=0, has_side_effects=True, vmem_limit_bytes=55 * 1024 * 1024
        ),
    )(
        view,
        facet_temp,
        emissivity,
        longwave_in,
        albedo,
        shortwave_in,
        dir_share.reshape(DIRS, width),
        vis_list,
        vis_mask,
        vis_source,
    )
    found = lax.cond(bad[0, 0] > 0, lambda: general(*args), lambda: found)
    width_out = 2 * points
    flux, radiant = pl.pallas_call(
        finish,
        grid=(tiles // 2,),
        out_shape=(
            jax.ShapeDtypeStruct((columns, tiles * points), jnp.float32),
            jax.ShapeDtypeStruct((HOURS, tiles * points), jnp.float32),
        ),
        in_specs=[pl.BlockSpec((columns, width_out), lambda i: (0, i))],
        out_specs=(
            pl.BlockSpec((columns, width_out), lambda i: (0, i)),
            pl.BlockSpec((HOURS, width_out), lambda i: (0, i)),
        ),
    )(found)
    return flux.reshape(DIRS, BANDS, HOURS, tiles * points), radiant


def solution(mesh):
    in_specs = (
        P(None, "tile", "blk"),
        P("tile", "blk"),
        P(None, "tile", "blk"),
        P("tile", "blk"),
        P(None, "tile", "blk"),
        P(None, "tile", "blk"),
        P("blk", "tile", None, None, None, None),
        P(("blk", "tile"), None),
        P(("blk", "tile"), None),
        P(("blk", "tile"), None),
    )
    out_specs = (P(None, None, None, ("blk", "tile")), P(None, ("blk", "tile")))
    return jax.shard_map(shards, mesh=mesh, in_specs=in_specs, out_specs=out_specs, check_vma=False)
```

```python
import functools

import jax
import jax.numpy as jnp
from jax import lax
from jax.experimental import pallas as pl
from jax.experimental.pallas import tpu as pltpu
from jax.sharding import PartitionSpec as P

DIRS = 6
BANDS = 2
HOURS = 48
NY = 4
NZ = 8
NT = NY * NZ
NB = 8
CUT = 4
DIR_WEIGHTS = (0.06, 0.06, 0.22, 0.22, 0.22, 0.22)
SHORT_FACTOR = 0.7 / 0.97
MESH = pl.DeviceIdType.MESH
RAD_ROWS = 112
FIRST_SENDS = 12
LOW_PER_COLUMN = 2
UNROLL = 8
LATE_LANE = 64
NEAR_AFTER = 1


def entry_slots(flat_mask, flat_source, tracer_count):
    tracer_ids = jnp.arange(tracer_count, dtype=jnp.int32)
    matching = (flat_source[:, None] == tracer_ids[None, :]).astype(jnp.int32)
    counted = matching * flat_mask[:, None]
    earlier = jnp.cumsum(counted, axis=0) - counted
    return jnp.sum(earlier * matching, axis=1)


def general(
    facet_temp,
    emissivity,
    longwave_in,
    albedo,
    shortwave_in,
    dir_share,
    view_blocks,
    vis_list,
    vis_mask,
    vis_source,
):
    long_rad = emissivity[None] * facet_temp**4 + (1.0 - emissivity[None]) * longwave_in
    short_rad = albedo[None] * shortwave_in
    radiosity = jnp.stack([long_rad, short_rad], 0).astype(jnp.bfloat16)
    local = jnp.concatenate(
        [radiosity.reshape(BANDS * HOURS, -1), dir_share.reshape(DIRS, -1)], axis=0
    )
    copies = jnp.broadcast_to(local[None], (lax.axis_size("blk"),) + local.shape)
    strip = lax.all_to_all(copies, "blk", split_axis=0, concat_axis=0, tiled=True)
    strip = jnp.transpose(strip, (1, 0, 2)).reshape(local.shape[0], -1).astype(jnp.float32)
    product = strip[BANDS * HOURS :, None, :] * strip[None, : BANDS * HOURS]
    strip_rows = product.astype(jnp.bfloat16).reshape(DIRS * BANDS * HOURS, -1)
    tracer_count = lax.axis_size("tile")
    capacity = view_blocks.shape[3]
    block_facets = view_blocks.shape[4]
    tile_points = view_blocks.shape[5]
    outgoing = view_blocks.reshape(tracer_count, capacity, block_facets, tile_points)
    received = lax.all_to_all(outgoing, "tile", split_axis=0, concat_axis=0, tiled=True)
    tiles_here, slot_count = vis_list.shape
    flat_mask = vis_mask.reshape(-1)
    flat_source = vis_source.reshape(-1)
    position = jnp.minimum(entry_slots(flat_mask, flat_source, tracer_count), capacity - 1)
    pick_index = flat_source * capacity + position
    blocks = received.reshape(tracer_count * capacity, block_facets, tile_points)[pick_index]
    blocks = blocks * flat_mask.astype(jnp.bfloat16)[:, None, None]
    blocks = blocks.reshape(tiles_here, slot_count * block_facets, tile_points)
    columns = strip_rows.shape[0]
    strip_blocks = strip_rows.reshape(columns, -1, block_facets)

    def one_tile(tile_args):
        tile_ids, tile_blocks = tile_args
        facet_rows = jnp.take(strip_blocks, tile_ids, axis=1).reshape(
            columns, slot_count * block_facets
        )
        return jnp.dot(facet_rows, tile_blocks, preferred_element_type=jnp.float32)

    per_tile = lax.map(one_tile, (vis_list, blocks))
    flux = jnp.transpose(per_tile, (1, 0, 2)).reshape(columns, tiles_here * tile_points)
    return flux


def within(index, size):
    return jnp.minimum(jnp.maximum(index, 0), size - 1)


def column_of(x):
    rows, width = x.shape
    eye = lax.broadcasted_iota(jnp.int32, (width, width), 0) == lax.broadcasted_iota(
        jnp.int32, (width, width), 1
    )
    parts = []
    for i in range(rows):
        line = jnp.broadcast_to(x[i : i + 1, :].astype(jnp.float32), (width, width))
        parts.append(jnp.sum(jnp.where(eye, line, 0.0), axis=1, keepdims=True))
    return jnp.concatenate(parts, axis=0)


def fill_flag(mask_ref, source_ref, flag):
    mask = column_of(mask_ref[...])
    source = column_of(source_ref[...])
    lane = lax.broadcasted_iota(jnp.int32, (mask.shape[0], 128), 1).astype(jnp.float32)
    named = jnp.sum(jnp.where((mask > 0.5) & (source == lane), 1.0, 0.0), axis=0, keepdims=True)
    most = jnp.max(named, axis=1, keepdims=True)
    flag[...] = jnp.broadcast_to(jnp.where(most > CUT + 0.5, 1, 0), flag.shape).astype(jnp.int32)


def fill_tables(last_row, list_ref, mask_ref, source_ref, table, ends):
    entries = mask_ref.shape[0] * mask_ref.shape[1]
    slots = mask_ref.shape[1]
    ids = column_of(list_ref[...])
    mask = column_of(mask_ref[...])
    source = column_of(source_ref[...])
    used = mask > 0.5
    entry = lax.broadcasted_iota(jnp.int32, (entries, 1), 0)
    tile = (entry // slots).astype(jnp.float32)
    before = (
        lax.broadcasted_iota(jnp.int32, (entries, entries), 1)
        < lax.broadcasted_iota(jnp.int32, (entries, entries), 0)
    ).astype(jnp.bfloat16)
    lane = lax.broadcasted_iota(jnp.int32, (entries, 128), 1).astype(jnp.float32)

    def earlier(chosen):
        count = jnp.dot(before, chosen.astype(jnp.bfloat16), preferred_element_type=jnp.float32)
        return jnp.sum(count * chosen, axis=1, keepdims=True)

    by_source = jnp.where(used & (source == lane), 1.0, 0.0)
    position = earlier(by_source)
    first = (last_row * NZ).astype(jnp.float32)
    late = (position == float(CUT - 1)) & (source >= first) & (source < first + float(NZ))
    group = jnp.where(late, float(2 * CUT), position)
    by_group = jnp.where(used & (group == lane), 1.0, 0.0)
    rank = earlier(by_group)
    place = jnp.where(late, float(CUT * NT - NZ), position * NT) + rank
    wide = lax.broadcasted_iota(jnp.int32, (entries, entries), 1).astype(jnp.float32)
    at = jnp.where(used & (place == wide), 1.0, 0.0)
    table[...] = jnp.zeros_like(table)
    table[0:1, :] = jnp.sum(at * ids, axis=0, keepdims=True).astype(jnp.int32)
    table[1:2, :] = jnp.sum(at * source, axis=0, keepdims=True).astype(jnp.int32)
    table[2:3, :] = jnp.sum(at * tile, axis=0, keepdims=True).astype(jnp.int32)
    up_to = jnp.where(tile <= lane, 1.0, 0.0)
    up_to_late = jnp.where(tile <= lane - LATE_LANE, 1.0, 0.0)
    for p in range(2 * CUT):
        chosen = jnp.sum(jnp.where(lane == float(p), by_group, 0.0), axis=1, keepdims=True)
        line = chosen * up_to
        if p == CUT - 1:
            chosen = jnp.sum(jnp.where(lane == float(2 * CUT), by_group, 0.0), axis=1, keepdims=True)
            line = jnp.where(lane < float(LATE_LANE), line, chosen * up_to_late)
        ends[p : p + 1, :] = jnp.sum(line, axis=0, keepdims=True).astype(jnp.int32)


def kernel(
    view, temp_hbm, emis_hbm, longwave_hbm, albedo_hbm, short_hbm, share_hbm, list_hbm, mask_hbm, source_hbm,
    flux, bad,
    low0, low1, low2, low3, low_late, high, near, rad, rows, running, table, ends, flag, flags, sums, pick, over, overs,
    table_s, ends_s, pick_s,
    low_send, low_recv, ring_send, ring_recv, col_send, col_recv, rad_send, rad_recv,
    flag_send, flag_recv, over_send, over_recv, local, row_here,
    temp_in, emis, longwave, albedo, short, share, list_ref, mask_ref, source_ref, loads,
):
    b = lax.axis_index("blk")
    t = lax.axis_index("tile")
    y = t // NZ
    z = lax.rem(t, NZ)

    def tile_peer(i):
        return lax.rem(y + i // NZ, NY) * NZ + lax.rem(z + lax.rem(i, NZ), NZ)

    barrier = pltpu.get_barrier_semaphore()

    for i in range(1, NZ):
        pl.semaphore_signal(barrier, inc=1, device_id=(b, tile_peer(i)), device_id_type=MESH)
    for i in range(NZ, NT, NZ):
        pl.semaphore_signal(barrier, inc=1, device_id=(b, tile_peer(i)), device_id_type=MESH)
    for i in range(1, NB):
        pl.semaphore_signal(
            barrier, inc=1, device_id=(lax.rem(b + i, NB), t), device_id_type=MESH
        )

    loading = [
        pltpu.make_async_copy(src, dst, loads.at[n])
        for n, (src, dst) in enumerate(
            (
                (temp_hbm, temp_in),
                (emis_hbm, emis),
                (longwave_hbm, longwave),
                (albedo_hbm, albedo),
                (short_hbm, short),
                (share_hbm, share),
                (list_hbm, list_ref),
                (mask_hbm, mask_ref),
                (source_hbm, source_ref),
            )
        )
    ]
    for n in (7, 8, 0, 1, 2, 3, 4, 5, 6):
        loading[n].start()
    high_copy = pltpu.make_async_copy(view.at[:, pl.ds(CUT, CUT)], high, local.at[0])
    low = (low0, low1, low2, low3)
    own_copies = [
        pltpu.make_async_copy(view.at[t, p], low[p].at[t], local.at[5 + p]) for p in range(CUT)
    ]

    loading[7].wait()
    loading[8].wait()
    fill_flag(mask_ref, source_ref, flag)
    flags[z] = flag[...]

    pl.semaphore_wait(barrier, NZ - 1 + NY - 1 + NB - 1)
    for i in range(NZ, NT, NZ):
        pl.semaphore_signal(row_here, inc=1, device_id=(b, tile_peer(i)), device_id_type=MESH)

    def flag_to(i):
        return pltpu.make_async_remote_copy(
            src_ref=flag, dst_ref=flags.at[z], send_sem=flag_send.at[i], recv_sem=flag_recv.at[i],
            device_id=(b, tile_peer(i)), device_id_type=MESH,
        )

    def sums_to(i):
        return pltpu.make_async_remote_copy(
            src_ref=sums.at[y], dst_ref=sums.at[y],
            send_sem=flag_send.at[NZ + i], recv_sem=flag_recv.at[NZ + i],
            device_id=(b, tile_peer(i * NZ)), device_id_type=MESH,
        )

    def rad_to(i):
        return pltpu.make_async_remote_copy(
            src_ref=rad.at[b], dst_ref=rad.at[b], send_sem=rad_send.at[i], recv_sem=rad_recv.at[i],
            device_id=(lax.rem(b + i, NB), t), device_id_type=MESH,
        )

    def low_to(p, i, late=False):
        return pltpu.make_async_remote_copy(
            src_ref=view.at[tile_peer(i), p], dst_ref=low_late.at[z] if late else low[p].at[t],
            send_sem=low_send.at[p, i], recv_sem=low_recv.at[p, i],
            device_id=(b, tile_peer(i)), device_id_type=MESH,
        )

    def over_to(i):
        return pltpu.make_async_remote_copy(
            src_ref=over, dst_ref=overs.at[b], send_sem=over_send.at[i], recv_sem=over_recv.at[i],
            device_id=(lax.rem(b + i, NB), t), device_id_type=MESH,
        )

    def ring_to(way, step):
        toward = lax.rem(z + (1, NZ - 1)[way], NZ)
        behind = y * NZ + lax.rem(z + (NZ - step, step)[way], NZ)
        half = CUT // 2
        part = pl.ds(0, CUT) if step < NZ // 2 - 1 else pl.ds(way * half, half)
        return pltpu.make_async_remote_copy(
            src_ref=near.at[behind, part], dst_ref=near.at[behind, part],
            send_sem=ring_send.at[way, step], recv_sem=ring_recv.at[way, step],
            device_id=(b, y * NZ + toward), device_id_type=MESH,
        )

    def column_to(dy, dz):
        held = y * NZ + lax.rem(z + dz, NZ)
        return pltpu.make_async_remote_copy(
            src_ref=near.at[held], dst_ref=near.at[held],
            send_sem=col_send.at[dy, dz], recv_sem=col_recv.at[dy, dz],
            device_id=(b, lax.rem(y + dy, NY) * NZ + z), device_id_type=MESH,
        )

    def looped(lo, hi, action):
        def body(i, carry):
            action(i)
            return carry

        lax.fori_loop(lo, hi, body, 0)

    sent = [1]

    def send_low(count):
        k = sent[0]
        end = min(CUT * NT, k + count)
        while k < end:
            p = k // NT
            stop = min(end, (p + 1) * NT)
            lo, hi = max(k - p * NT, 1), stop - p * NT
            split = NT - NZ if p == CUT - 1 else NT
            if lo < split:
                looped(lo, min(hi, split), lambda i: low_to(p, i).start())
            if hi > split:
                looped(max(lo, split), hi, lambda i: low_to(p, i, True).start())
            k = stop
        sent[0] = k

    for i in range(1, NZ):
        flag_to(i).start()
    send_low(NZ - 1)
    high_copy.start()
    pl.semaphore_wait(row_here, NY - 1)
    send_low(FIRST_SENDS // 2)

    for copy in loading[:7]:
        copy.wait()
    emissivity = emis[...]
    long_rad = emissivity * temp_in[:, 0, :] ** 4 + (1.0 - emissivity) * longwave[:, 0, :]
    rad[b, 0:HOURS, :] = long_rad.astype(jnp.bfloat16)
    rad[b, HOURS : 2 * HOURS, :] = (albedo[...] * short[:, 0, :]).astype(jnp.bfloat16)
    rad[b, 2 * HOURS : RAD_ROWS, :] = jnp.concatenate(
        [share[...].astype(jnp.float32), jnp.zeros((RAD_ROWS - 2 * HOURS - DIRS, share.shape[1]), jnp.float32)],
        axis=0,
    ).astype(jnp.bfloat16)

    for i in range(1, NZ):
        flag_to(i).wait()
    total = jnp.zeros((8, 128), jnp.int32)
    where_to = jnp.zeros((8, 128), jnp.int32)
    for o in range(NZ):
        total += flags[o]
        where_to += flags[o] * (y * NZ + o)
    sums[y, 0] = total
    sums[y, 1] = where_to
    for i in range(1, NY):
        sums_to(i).start()
    send_low(FIRST_SENDS // 2)
    looped(1, NB, lambda i: rad_to(i).start())
    for i in range(1, NY):
        sums_to(i).wait()
    total = sums[0, 0]
    where_to = sums[0, 1]
    for i in range(1, NY):
        total += sums[i, 0]
        where_to += sums[i, 1]
    pick[...] = jnp.where(total == 1, where_to, 0)
    over[...] = jnp.where(total > 1, 1, 0).astype(jnp.int32)
    overs[b] = over[...]
    pick_copy = pltpu.make_async_copy(pick, pick_s, local.at[4])
    pick_copy.start()
    looped(1, NB, lambda i: over_to(i).start())
    high_copy.wait()
    pick_copy.wait()
    near[t] = high[within(pick_s[0, 0], NT)]
    for copy in own_copies:
        copy.start()

    for step in range(NZ // 2):
        ring_to(0, step).start()
        ring_to(1, step).start()
        if step == 0:
            shares = [0]
        else:
            shares = [step, NZ - step]
        for dz in shares:
            for dy in range(1, NY):
                column_to(dy, dz).start()
                send_low(LOW_PER_COLUMN)
        ring_to(0, step).wait()
        ring_to(1, step).wait()
    for dy in range(1, NY):
        column_to(dy, NZ // 2).start()
        send_low(LOW_PER_COLUMN)
    send_low(CUT * NT)

    running[0] = jnp.zeros(running.shape[1:], jnp.float32)
    fill_tables(lax.rem(y + 1, NY), list_ref, mask_ref, source_ref, table, ends)
    table_copy = pltpu.make_async_copy(table, table_s, local.at[2])
    table_copy.start()
    ends_copy = pltpu.make_async_copy(ends, ends_s, local.at[3])
    ends_copy.start()
    for copy in own_copies:
        copy.wait()
    table_copy.wait()
    ends_copy.wait()
    looped(1, NB, lambda i: rad_to(i).wait())

    facet_blocks = rad.shape[2] // 128

    def weight(j, carry):
        for q in range(facet_blocks):
            cols = slice(q * 128, (q + 1) * 128)
            radiosity = rad[j, 0 : 2 * HOURS, cols].astype(jnp.float32)
            shares = rad[j, 2 * HOURS : RAD_ROWS, cols].astype(jnp.float32)
            for d in range(DIRS):
                rows[j * facet_blocks + q, d * 2 * HOURS : (d + 1) * 2 * HOURS, :] = (
                    shares[d : d + 1, :] * radiosity
                ).astype(jnp.bfloat16)
        return carry

    lax.fori_loop(0, NB, weight, 0)

    tiles = mask_ref.shape[0]

    def group_products(p, base, count, held, first_phase, lane=0):
        def body(turn, carry):
            for u in range(UNROLL):
                r = turn * UNROLL + u
                g = base + r
                same = (r > 0) & (table_s[2, g] == table_s[2, jnp.maximum(g - 1, 0)])
                product = jnp.dot(
                    rows[within(table_s[0, g], rows.shape[0])],
                    held(within(table_s[1, g], NT)),
                    preferred_element_type=jnp.float32,
                )
                running[r + 1] = product + jnp.where(same, running[r], 0.0)
            return carry

        lax.fori_loop(0, count // UNROLL, body, 0)
        for i in range(tiles):
            end = within(ends_s[p, lane + i], NT + 1)
            start = within(ends_s[p, lane + i - 1], NT + 1) if i else 0
            cols = slice(i * 128, (i + 1) * 128)
            part = jnp.where(end > start, running[end], 0.0)
            if first_phase:
                flux[:, cols] = part
            else:
                flux[:, cols] += part

    def low_wait(p, lo, hi, late=False):
        looped(lo, hi, lambda i: low_to(p, i, late).wait())

    def near_products():
        for dy in range(1, NY):
            looped(0, NZ, lambda dz: column_to(dy, dz).wait())
        for q in range(CUT):
            group_products(CUT + q, (CUT + q) * NT, NT, lambda s: near[s, q], False)

    looped(1, NB, lambda i: over_to(i).wait())
    any_over = overs[0]
    for i in range(1, NB):
        any_over += overs[i]
    over[...] = any_over
    over_copy = pltpu.make_async_copy(over, pick_s, local.at[4])
    over_copy.start()
    over_copy.wait()
    bad[0, 0] = pick_s[0, 0]

    for p in range(CUT - 1):
        low_wait(p, 1, NT)
        group_products(p, p * NT, NT, lambda s: low[p][s], p == 0)
        if p == NEAR_AFTER:
            near_products()
    p = CUT - 1
    low_wait(p, 1, NT - NZ)
    group_products(p, p * NT, NT - NZ, lambda s: low[p][s], False)
    low_wait(p, NT - NZ, NT, True)
    group_products(p, CUT * NT - NZ, NZ, lambda s: low_late[lax.rem(s, NZ)], False, LATE_LANE)


def finish(found, flux, radiant):
    total = None
    for d in range(DIRS):
        base = d * 2 * HOURS
        part = DIR_WEIGHTS[d] * (
            found[base : base + HOURS, :] + SHORT_FACTOR * found[base + HOURS : base + 2 * HOURS, :]
        )
        total = part if total is None else total + part
    radiant[...] = jnp.sqrt(jnp.sqrt(total))
    flux[...] = found[...]


def shards(*args):
    (facet_temp, emissivity, longwave_in, albedo, shortwave_in, dir_share, view_blocks,
     vis_list, vis_mask, vis_source) = args
    width = facet_temp.shape[2]
    capacity, facets, points = view_blocks.shape[3:]
    tiles, slots = vis_list.shape
    columns = DIRS * BANDS * HOURS
    assert capacity == 2 * CUT and tiles * slots == capacity * NT
    view = view_blocks.reshape(NT, capacity, facets, points)
    operands = (
        facet_temp,
        emissivity,
        longwave_in,
        albedo,
        shortwave_in,
        dir_share.reshape(DIRS, width),
        vis_list,
        vis_mask,
        vis_source,
    )
    vmem = pl.BlockSpec(memory_space=pltpu.VMEM)
    dma = pltpu.SemaphoreType.DMA
    found, bad = pl.pallas_call(
        kernel,
        out_shape=(
            jax.ShapeDtypeStruct((columns, tiles * points), jnp.float32),
            jax.ShapeDtypeStruct((1, 1), jnp.int32),
        ),
        in_specs=[pl.BlockSpec(memory_space=pl.ANY)] * 10,
        out_specs=(vmem, pl.BlockSpec(memory_space=pltpu.SMEM)),
        scratch_shapes=[
            *([pltpu.VMEM((NT, facets, points), jnp.bfloat16)] * CUT),
            pltpu.VMEM((NZ, facets, points), jnp.bfloat16),
            pltpu.VMEM((NT, CUT, facets, points), jnp.bfloat16),
            pltpu.VMEM((NT, CUT, facets, points), jnp.bfloat16),
            pltpu.VMEM((NB, RAD_ROWS, width), jnp.bfloat16),
            pltpu.VMEM((NB * width // facets, columns, facets), jnp.bfloat16),
            pltpu.VMEM((NT + 1, columns, points), jnp.float32),
            pltpu.VMEM((8, tiles * slots), jnp.int32),
            pltpu.VMEM((8, 128), jnp.int32),
            pltpu.VMEM((8, 128), jnp.int32),
            pltpu.VMEM((NZ, 8, 128), jnp.int32),
            pltpu.VMEM((NY, 2, 8, 128), jnp.int32),
            pltpu.VMEM((8, 128), jnp.int32),
            pltpu.VMEM((8, 128), jnp.int32),
            pltpu.VMEM((NB, 8, 128), jnp.int32),
            pltpu.SMEM((8, tiles * slots), jnp.int32),
            pltpu.SMEM((8, 128), jnp.int32),
            pltpu.SMEM((8, 128), jnp.int32),
            dma((CUT, NT)),
            dma((CUT, NT)),
            dma((2, NZ // 2)),
            dma((2, NZ // 2)),
            dma((NY, NZ)),
            dma((NY, NZ)),
            dma((NB,)),
            dma((NB,)),
            dma((NT,)),
            dma((NT,)),
            dma((NB,)),
            dma((NB,)),
            dma((5 + CUT,)),
            pltpu.SemaphoreType.REGULAR,
            *[pltpu.VMEM(x.shape, x.dtype) for x in operands],
            dma((len(operands),)),
        ],
        compiler_params=pltpu.CompilerParams(
            collective_id=0, has_side_effects=True, vmem_limit_bytes=55 * 1024 * 1024
        ),
    )(view, *operands)
    found = lax.cond(bad[0, 0] > 0, lambda: general(*args), lambda: found)
    width_out = 2 * points
    flux, radiant = pl.pallas_call(
        finish,
        grid=(tiles // 2,),
        out_shape=(
            jax.ShapeDtypeStruct((columns, tiles * points), jnp.float32),
            jax.ShapeDtypeStruct((HOURS, tiles * points), jnp.float32),
        ),
        in_specs=[pl.BlockSpec((columns, width_out), lambda i: (0, i))],
        out_specs=(
            pl.BlockSpec((columns, width_out), lambda i: (0, i)),
            pl.BlockSpec((HOURS, width_out), lambda i: (0, i)),
        ),
    )(found)
    return flux.reshape(DIRS, BANDS, HOURS, tiles * points), radiant


def solution(mesh):
    in_specs = (
        P(None, "tile", "blk"),
        P("tile", "blk"),
        P(None, "tile", "blk"),
        P("tile", "blk"),
        P(None, "tile", "blk"),
        P(None, "tile", "blk"),
        P("blk", "tile", None, None, None, None),
        P(("blk", "tile"), None),
        P(("blk", "tile"), None),
        P(("blk", "tile"), None),
    )
    out_specs = (P(None, None, None, ("blk", "tile")), P(None, ("blk", "tile")))
    return jax.shard_map(shards, mesh=mesh, in_specs=in_specs, out_specs=out_specs, check_vma=False)
```

```python
import functools

import jax
import jax.numpy as jnp
from jax import lax
from jax.experimental import pallas as pl
from jax.experimental.pallas import tpu as pltpu
from jax.sharding import PartitionSpec as P

DIRS = 6
BANDS = 2
HOURS = 48
NY = 4
NZ = 8
NT = NY * NZ
NB = 8
CUT = 4
DIR_WEIGHTS = (0.06, 0.06, 0.22, 0.22, 0.22, 0.22)
SHORT_FACTOR = 0.7 / 0.97
MESH = pl.DeviceIdType.MESH
RAD_ROWS = 112
FIRST_SENDS = 12
LOW_PER_COLUMN = 2
UNROLL = 8
LATE_LANE = 64
NEAR_AFTER = 1


def entry_slots(flat_mask, flat_source, tracer_count):
    tracer_ids = jnp.arange(tracer_count, dtype=jnp.int32)
    matching = (flat_source[:, None] == tracer_ids[None, :]).astype(jnp.int32)
    counted = matching * flat_mask[:, None]
    earlier = jnp.cumsum(counted, axis=0) - counted
    return jnp.sum(earlier * matching, axis=1)


def general(
    facet_temp,
    emissivity,
    longwave_in,
    albedo,
    shortwave_in,
    dir_share,
    view_blocks,
    vis_list,
    vis_mask,
    vis_source,
):
    long_rad = emissivity[None] * facet_temp**4 + (1.0 - emissivity[None]) * longwave_in
    short_rad = albedo[None] * shortwave_in
    radiosity = jnp.stack([long_rad, short_rad], 0).astype(jnp.bfloat16)
    local = jnp.concatenate(
        [radiosity.reshape(BANDS * HOURS, -1), dir_share.reshape(DIRS, -1)], axis=0
    )
    copies = jnp.broadcast_to(local[None], (lax.axis_size("blk"),) + local.shape)
    strip = lax.all_to_all(copies, "blk", split_axis=0, concat_axis=0, tiled=True)
    strip = jnp.transpose(strip, (1, 0, 2)).reshape(local.shape[0], -1).astype(jnp.float32)
    product = strip[BANDS * HOURS :, None, :] * strip[None, : BANDS * HOURS]
    strip_rows = product.astype(jnp.bfloat16).reshape(DIRS * BANDS * HOURS, -1)
    tracer_count = lax.axis_size("tile")
    capacity = view_blocks.shape[3]
    block_facets = view_blocks.shape[4]
    tile_points = view_blocks.shape[5]
    outgoing = view_blocks.reshape(tracer_count, capacity, block_facets, tile_points)
    received = lax.all_to_all(outgoing, "tile", split_axis=0, concat_axis=0, tiled=True)
    tiles_here, slot_count = vis_list.shape
    flat_mask = vis_mask.reshape(-1)
    flat_source = vis_source.reshape(-1)
    position = jnp.minimum(entry_slots(flat_mask, flat_source, tracer_count), capacity - 1)
    pick_index = flat_source * capacity + position
    blocks = received.reshape(tracer_count * capacity, block_facets, tile_points)[pick_index]
    blocks = blocks * flat_mask.astype(jnp.bfloat16)[:, None, None]
    blocks = blocks.reshape(tiles_here, slot_count * block_facets, tile_points)
    columns = strip_rows.shape[0]
    strip_blocks = strip_rows.reshape(columns, -1, block_facets)

    def one_tile(tile_args):
        tile_ids, tile_blocks = tile_args
        facet_rows = jnp.take(strip_blocks, tile_ids, axis=1).reshape(
            columns, slot_count * block_facets
        )
        return jnp.dot(facet_rows, tile_blocks, preferred_element_type=jnp.float32)

    per_tile = lax.map(one_tile, (vis_list, blocks))
    flux = jnp.transpose(per_tile, (1, 0, 2)).reshape(columns, tiles_here * tile_points)
    return flux


def within(index, size):
    return jnp.minimum(jnp.maximum(index, 0), size - 1)


def column_of(x):
    rows, width = x.shape
    eye = lax.broadcasted_iota(jnp.int32, (width, width), 0) == lax.broadcasted_iota(
        jnp.int32, (width, width), 1
    )
    parts = []
    for i in range(rows):
        line = jnp.broadcast_to(x[i : i + 1, :].astype(jnp.float32), (width, width))
        parts.append(jnp.sum(jnp.where(eye, line, 0.0), axis=1, keepdims=True))
    return jnp.concatenate(parts, axis=0)


def fill_flag(mask_ref, source_ref, flag):
    mask = column_of(mask_ref[...])
    source = column_of(source_ref[...])
    lane = lax.broadcasted_iota(jnp.int32, (mask.shape[0], 128), 1).astype(jnp.float32)
    named = jnp.sum(jnp.where((mask > 0.5) & (source == lane), 1.0, 0.0), axis=0, keepdims=True)
    most = jnp.max(named, axis=1, keepdims=True)
    flag[...] = jnp.broadcast_to(jnp.where(most > CUT + 0.5, 1, 0), flag.shape).astype(jnp.int32)


def fill_tables(last_row, list_ref, mask_ref, source_ref, table, ends):
    entries = mask_ref.shape[0] * mask_ref.shape[1]
    slots = mask_ref.shape[1]
    ids = column_of(list_ref[...])
    mask = column_of(mask_ref[...])
    source = column_of(source_ref[...])
    used = mask > 0.5
    entry = lax.broadcasted_iota(jnp.int32, (entries, 1), 0)
    tile = (entry // slots).astype(jnp.float32)
    before = (
        lax.broadcasted_iota(jnp.int32, (entries, entries), 1)
        < lax.broadcasted_iota(jnp.int32, (entries, entries), 0)
    ).astype(jnp.bfloat16)
    lane = lax.broadcasted_iota(jnp.int32, (entries, 128), 1).astype(jnp.float32)

    def earlier(chosen):
        count = jnp.dot(before, chosen.astype(jnp.bfloat16), preferred_element_type=jnp.float32)
        return jnp.sum(count * chosen, axis=1, keepdims=True)

    by_source = jnp.where(used & (source == lane), 1.0, 0.0)
    position = earlier(by_source)
    first = (last_row * NZ).astype(jnp.float32)
    late = (position == float(CUT - 1)) & (source >= first) & (source < first + float(NZ))
    group = jnp.where(late, float(2 * CUT), position)
    by_group = jnp.where(used & (group == lane), 1.0, 0.0)
    rank = earlier(by_group)
    place = jnp.where(late, float(CUT * NT - NZ), position * NT) + rank
    wide = lax.broadcasted_iota(jnp.int32, (entries, entries), 1).astype(jnp.float32)
    at = jnp.where(used & (place == wide), 1.0, 0.0)
    table[...] = jnp.zeros_like(table)
    table[0:1, :] = jnp.sum(at * ids, axis=0, keepdims=True).astype(jnp.int32)
    table[1:2, :] = jnp.sum(at * source, axis=0, keepdims=True).astype(jnp.int32)
    table[2:3, :] = jnp.sum(at * tile, axis=0, keepdims=True).astype(jnp.int32)
    up_to = jnp.where(tile <= lane, 1.0, 0.0)
    up_to_late = jnp.where(tile <= lane - LATE_LANE, 1.0, 0.0)
    for p in range(2 * CUT):
        chosen = jnp.sum(jnp.where(lane == float(p), by_group, 0.0), axis=1, keepdims=True)
        line = chosen * up_to
        if p == CUT - 1:
            chosen = jnp.sum(jnp.where(lane == float(2 * CUT), by_group, 0.0), axis=1, keepdims=True)
            line = jnp.where(lane < float(LATE_LANE), line, chosen * up_to_late)
        ends[p : p + 1, :] = jnp.sum(line, axis=0, keepdims=True).astype(jnp.int32)


def kernel(
    view, temp_hbm, emis_hbm, longwave_hbm, albedo_hbm, short_hbm, share_hbm, list_hbm, mask_hbm, source_hbm,
    flux, bad,
    low0, low1, low2, low3, low_late, high, near, rad, rows, running, table, ends, flag, flags, sums, pick, over, overs,
    table_s, ends_s, pick_s,
    low_send, low_recv, ring_send, ring_recv, col_send, col_recv, rad_send, rad_recv,
    flag_send, flag_recv, over_send, over_recv, local, row_here,
    temp_in, emis, longwave, albedo, short, share, list_ref, mask_ref, source_ref, loads,
):
    b = lax.axis_index("blk")
    t = lax.axis_index("tile")
    y = t // NZ
    z = lax.rem(t, NZ)

    def tile_peer(i):
        j = lax.rem(i, NZ)
        odd = lax.rem(j, 2)
        half = NZ // 2
        dz = odd * (half + j // 2) + (1 - odd) * (half - j // 2) * ((j + NZ - 1) // NZ)
        return lax.rem(y + i // NZ, NY) * NZ + lax.rem(z + dz, NZ)

    barrier = pltpu.get_barrier_semaphore()

    for i in range(1, NZ):
        pl.semaphore_signal(barrier, inc=1, device_id=(b, tile_peer(i)), device_id_type=MESH)
    for i in range(NZ, NT, NZ):
        pl.semaphore_signal(barrier, inc=1, device_id=(b, tile_peer(i)), device_id_type=MESH)
    for i in range(1, NB):
        pl.semaphore_signal(
            barrier, inc=1, device_id=(lax.rem(b + i, NB), t), device_id_type=MESH
        )

    loading = [
        pltpu.make_async_copy(src, dst, loads.at[n])
        for n, (src, dst) in enumerate(
            (
                (temp_hbm, temp_in),
                (emis_hbm, emis),
                (longwave_hbm, longwave),
                (albedo_hbm, albedo),
                (short_hbm, short),
                (share_hbm, share),
                (list_hbm, list_ref),
                (mask_hbm, mask_ref),
                (source_hbm, source_ref),
            )
        )
    ]
    for n in (7, 8, 0, 1, 2, 3, 4, 5, 6):
        loading[n].start()
    high_copy = pltpu.make_async_copy(view.at[:, pl.ds(CUT, CUT)], high, local.at[0])
    low = (low0, low1, low2, low3)
    own_copies = [
        pltpu.make_async_copy(view.at[t, p], low[p].at[t], local.at[5 + p]) for p in range(CUT)
    ]

    loading[7].wait()
    loading[8].wait()
    fill_flag(mask_ref, source_ref, flag)
    flags[z] = flag[...]

    pl.semaphore_wait(barrier, NZ - 1 + NY - 1 + NB - 1)
    for i in range(NZ, NT, NZ):
        pl.semaphore_signal(row_here, inc=1, device_id=(b, tile_peer(i)), device_id_type=MESH)

    def flag_to(i):
        return pltpu.make_async_remote_copy(
            src_ref=flag, dst_ref=flags.at[z], send_sem=flag_send.at[i], recv_sem=flag_recv.at[i],
            device_id=(b, tile_peer(i)), device_id_type=MESH,
        )

    def sums_to(i):
        return pltpu.make_async_remote_copy(
            src_ref=sums.at[y], dst_ref=sums.at[y],
            send_sem=flag_send.at[NZ + i], recv_sem=flag_recv.at[NZ + i],
            device_id=(b, tile_peer(i * NZ)), device_id_type=MESH,
        )

    def rad_to(i):
        return pltpu.make_async_remote_copy(
            src_ref=rad.at[b], dst_ref=rad.at[b], send_sem=rad_send.at[i], recv_sem=rad_recv.at[i],
            device_id=(lax.rem(b + i, NB), t), device_id_type=MESH,
        )

    def low_to(p, i, late=False):
        return pltpu.make_async_remote_copy(
            src_ref=view.at[tile_peer(i), p], dst_ref=low_late.at[z] if late else low[p].at[t],
            send_sem=low_send.at[p, i], recv_sem=low_recv.at[p, i],
            device_id=(b, tile_peer(i)), device_id_type=MESH,
        )

    def over_to(i):
        return pltpu.make_async_remote_copy(
            src_ref=over, dst_ref=overs.at[b], send_sem=over_send.at[i], recv_sem=over_recv.at[i],
            device_id=(lax.rem(b + i, NB), t), device_id_type=MESH,
        )

    def ring_to(way, step):
        toward = lax.rem(z + (1, NZ - 1)[way], NZ)
        behind = y * NZ + lax.rem(z + (NZ - step, step)[way], NZ)
        half = CUT // 2
        part = pl.ds(0, CUT) if step < NZ // 2 - 1 else pl.ds(way * half, half)
        return pltpu.make_async_remote_copy(
            src_ref=near.at[behind, part], dst_ref=near.at[behind, part],
            send_sem=ring_send.at[way, step], recv_sem=ring_recv.at[way, step],
            device_id=(b, y * NZ + toward), device_id_type=MESH,
        )

    def column_to(dy, dz):
        held = y * NZ + lax.rem(z + dz, NZ)
        return pltpu.make_async_remote_copy(
            src_ref=near.at[held], dst_ref=near.at[held],
            send_sem=col_send.at[dy, dz], recv_sem=col_recv.at[dy, dz],
            device_id=(b, lax.rem(y + dy, NY) * NZ + z), device_id_type=MESH,
        )

    def looped(lo, hi, action):
        def body(i, carry):
            action(i)
            return carry

        lax.fori_loop(lo, hi, body, 0)

    sent = [1]

    def send_low(count):
        k = sent[0]
        end = min(CUT * NT, k + count)
        while k < end:
            p = k // NT
            stop = min(end, (p + 1) * NT)
            lo, hi = max(k - p * NT, 1), stop - p * NT
            split = NT - NZ if p == CUT - 1 else NT
            if lo < split:
                looped(lo, min(hi, split), lambda i: low_to(p, i).start())
            if hi > split:
                looped(max(lo, split), hi, lambda i: low_to(p, i, True).start())
            k = stop
        sent[0] = k

    for i in range(1, NZ):
        flag_to(i).start()
    send_low(NZ - 1)
    high_copy.start()
    pl.semaphore_wait(row_here, NY - 1)
    send_low(FIRST_SENDS // 2)

    for copy in loading[:7]:
        copy.wait()
    emissivity = emis[...]
    long_rad = emissivity * temp_in[:, 0, :] ** 4 + (1.0 - emissivity) * longwave[:, 0, :]
    rad[b, 0:HOURS, :] = long_rad.astype(jnp.bfloat16)
    rad[b, HOURS : 2 * HOURS, :] = (albedo[...] * short[:, 0, :]).astype(jnp.bfloat16)
    rad[b, 2 * HOURS : RAD_ROWS, :] = jnp.concatenate(
        [share[...].astype(jnp.float32), jnp.zeros((RAD_ROWS - 2 * HOURS - DIRS, share.shape[1]), jnp.float32)],
        axis=0,
    ).astype(jnp.bfloat16)

    for i in range(1, NZ):
        flag_to(i).wait()
    total = jnp.zeros((8, 128), jnp.int32)
    where_to = jnp.zeros((8, 128), jnp.int32)
    for o in range(NZ):
        total += flags[o]
        where_to += flags[o] * (y * NZ + o)
    sums[y, 0] = total
    sums[y, 1] = where_to
    for i in range(1, NY):
        sums_to(i).start()
    send_low(FIRST_SENDS // 2)
    looped(1, NB, lambda i: rad_to(i).start())
    for i in range(1, NY):
        sums_to(i).wait()
    total = sums[0, 0]
    where_to = sums[0, 1]
    for i in range(1, NY):
        total += sums[i, 0]
        where_to += sums[i, 1]
    pick[...] = jnp.where(total == 1, where_to, 0)
    over[...] = jnp.where(total > 1, 1, 0).astype(jnp.int32)
    overs[b] = over[...]
    pick_copy = pltpu.make_async_copy(pick, pick_s, local.at[4])
    pick_copy.start()
    looped(1, NB, lambda i: over_to(i).start())
    high_copy.wait()
    pick_copy.wait()
    near[t] = high[within(pick_s[0, 0], NT)]
    for copy in own_copies:
        copy.start()

    for step in range(NZ // 2):
        ring_to(0, step).start()
        ring_to(1, step).start()
        if step == 0:
            shares = [0]
        else:
            shares = [step, NZ - step]
        for dz in shares:
            for dy in range(1, NY):
                column_to(dy, dz).start()
                send_low(LOW_PER_COLUMN)
        ring_to(0, step).wait()
        ring_to(1, step).wait()
    for dy in range(1, NY):
        column_to(dy, NZ // 2).start()
        send_low(LOW_PER_COLUMN)
    send_low(CUT * NT)

    running[0] = jnp.zeros(running.shape[1:], jnp.float32)
    fill_tables(lax.rem(y + 1, NY), list_ref, mask_ref, source_ref, table, ends)
    table_copy = pltpu.make_async_copy(table, table_s, local.at[2])
    table_copy.start()
    ends_copy = pltpu.make_async_copy(ends, ends_s, local.at[3])
    ends_copy.start()
    for copy in own_copies:
        copy.wait()
    table_copy.wait()
    ends_copy.wait()
    looped(1, NB, lambda i: rad_to(i).wait())

    facet_blocks = rad.shape[2] // 128

    def weight(j, carry):
        for q in range(facet_blocks):
            cols = slice(q * 128, (q + 1) * 128)
            radiosity = rad[j, 0 : 2 * HOURS, cols].astype(jnp.float32)
            shares = rad[j, 2 * HOURS : RAD_ROWS, cols].astype(jnp.float32)
            for d in range(DIRS):
                rows[j * facet_blocks + q, d * 2 * HOURS : (d + 1) * 2 * HOURS, :] = (
                    shares[d : d + 1, :] * radiosity
                ).astype(jnp.bfloat16)
        return carry

    lax.fori_loop(0, NB, weight, 0)

    tiles = mask_ref.shape[0]

    def group_products(p, base, count, held, first_phase, lane=0):
        def body(turn, carry):
            for u in range(UNROLL):
                r = turn * UNROLL + u
                g = base + r
                same = (r > 0) & (table_s[2, g] == table_s[2, jnp.maximum(g - 1, 0)])
                product = jnp.dot(
                    rows[within(table_s[0, g], rows.shape[0])],
                    held(within(table_s[1, g], NT)),
                    preferred_element_type=jnp.float32,
                )
                running[r + 1] = product + jnp.where(same, running[r], 0.0)
            return carry

        lax.fori_loop(0, count // UNROLL, body, 0)
        for i in range(tiles):
            end = within(ends_s[p, lane + i], NT + 1)
            start = within(ends_s[p, lane + i - 1], NT + 1) if i else 0
            cols = slice(i * 128, (i + 1) * 128)
            part = jnp.where(end > start, running[end], 0.0)
            if first_phase:
                flux[:, cols] = part
            else:
                flux[:, cols] += part

    def low_wait(p, lo, hi, late=False):
        looped(lo, hi, lambda i: low_to(p, i, late).wait())

    def near_products():
        for dy in range(1, NY):
            looped(0, NZ, lambda dz: column_to(dy, dz).wait())
        for q in range(CUT):
            group_products(CUT + q, (CUT + q) * NT, NT, lambda s: near[s, q], False)

    looped(1, NB, lambda i: over_to(i).wait())
    any_over = overs[0]
    for i in range(1, NB):
        any_over += overs[i]
    over[...] = any_over
    over_copy = pltpu.make_async_copy(over, pick_s, local.at[4])
    over_copy.start()
    over_copy.wait()
    bad[0, 0] = pick_s[0, 0]

    for p in range(CUT - 1):
        low_wait(p, 1, NT)
        group_products(p, p * NT, NT, lambda s: low[p][s], p == 0)
        if p == NEAR_AFTER:
            near_products()
    p = CUT - 1
    low_wait(p, 1, NT - NZ)
    group_products(p, p * NT, NT - NZ, lambda s: low[p][s], False)
    low_wait(p, NT - NZ, NT, True)
    group_products(p, CUT * NT - NZ, NZ, lambda s: low_late[lax.rem(s, NZ)], False, LATE_LANE)


def finish(found, flux, radiant):
    total = None
    for d in range(DIRS):
        base = d * 2 * HOURS
        part = DIR_WEIGHTS[d] * (
            found[base : base + HOURS, :] + SHORT_FACTOR * found[base + HOURS : base + 2 * HOURS, :]
        )
        total = part if total is None else total + part
    radiant[...] = jnp.sqrt(jnp.sqrt(total))
    flux[...] = found[...]


def shards(*args):
    (facet_temp, emissivity, longwave_in, albedo, shortwave_in, dir_share, view_blocks,
     vis_list, vis_mask, vis_source) = args
    width = facet_temp.shape[2]
    capacity, facets, points = view_blocks.shape[3:]
    tiles, slots = vis_list.shape
    columns = DIRS * BANDS * HOURS
    assert capacity == 2 * CUT and tiles * slots == capacity * NT
    view = view_blocks.reshape(NT, capacity, facets, points)
    operands = (
        facet_temp,
        emissivity,
        longwave_in,
        albedo,
        shortwave_in,
        dir_share.reshape(DIRS, width),
        vis_list,
        vis_mask,
        vis_source,
    )
    vmem = pl.BlockSpec(memory_space=pltpu.VMEM)
    dma = pltpu.SemaphoreType.DMA
    found, bad = pl.pallas_call(
        kernel,
        out_shape=(
            jax.ShapeDtypeStruct((columns, tiles * points), jnp.float32),
            jax.ShapeDtypeStruct((1, 1), jnp.int32),
        ),
        in_specs=[pl.BlockSpec(memory_space=pl.ANY)] * 10,
        out_specs=(vmem, pl.BlockSpec(memory_space=pltpu.SMEM)),
        scratch_shapes=[
            *([pltpu.VMEM((NT, facets, points), jnp.bfloat16)] * CUT),
            pltpu.VMEM((NZ, facets, points), jnp.bfloat16),
            pltpu.VMEM((NT, CUT, facets, points), jnp.bfloat16),
            pltpu.VMEM((NT, CUT, facets, points), jnp.bfloat16),
            pltpu.VMEM((NB, RAD_ROWS, width), jnp.bfloat16),
            pltpu.VMEM((NB * width // facets, columns, facets), jnp.bfloat16),
            pltpu.VMEM((NT + 1, columns, points), jnp.float32),
            pltpu.VMEM((8, tiles * slots), jnp.int32),
            pltpu.VMEM((8, 128), jnp.int32),
            pltpu.VMEM((8, 128), jnp.int32),
            pltpu.VMEM((NZ, 8, 128), jnp.int32),
            pltpu.VMEM((NY, 2, 8, 128), jnp.int32),
            pltpu.VMEM((8, 128), jnp.int32),
            pltpu.VMEM((8, 128), jnp.int32),
            pltpu.VMEM((NB, 8, 128), jnp.int32),
            pltpu.SMEM((8, tiles * slots), jnp.int32),
            pltpu.SMEM((8, 128), jnp.int32),
            pltpu.SMEM((8, 128), jnp.int32),
            dma((CUT, NT)),
            dma((CUT, NT)),
            dma((2, NZ // 2)),
            dma((2, NZ // 2)),
            dma((NY, NZ)),
            dma((NY, NZ)),
            dma((NB,)),
            dma((NB,)),
            dma((NT,)),
            dma((NT,)),
            dma((NB,)),
            dma((NB,)),
            dma((5 + CUT,)),
            pltpu.SemaphoreType.REGULAR,
            *[pltpu.VMEM(x.shape, x.dtype) for x in operands],
            dma((len(operands),)),
        ],
        compiler_params=pltpu.CompilerParams(
            collective_id=0, has_side_effects=True, vmem_limit_bytes=55 * 1024 * 1024
        ),
    )(view, *operands)
    found = lax.cond(bad[0, 0] > 0, lambda: general(*args), lambda: found)
    width_out = 4 * points
    flux, radiant = pl.pallas_call(
        finish,
        grid=(tiles // 4,),
        out_shape=(
            jax.ShapeDtypeStruct((columns, tiles * points), jnp.float32),
            jax.ShapeDtypeStruct((HOURS, tiles * points), jnp.float32),
        ),
        in_specs=[pl.BlockSpec((columns, width_out), lambda i: (0, i))],
        out_specs=(
            pl.BlockSpec((columns, width_out), lambda i: (0, i)),
            pl.BlockSpec((HOURS, width_out), lambda i: (0, i)),
        ),
    )(found)
    return flux.reshape(DIRS, BANDS, HOURS, tiles * points), radiant


def solution(mesh):
    in_specs = (
        P(None, "tile", "blk"),
        P("tile", "blk"),
        P(None, "tile", "blk"),
        P("tile", "blk"),
        P(None, "tile", "blk"),
        P(None, "tile", "blk"),
        P("blk", "tile", None, None, None, None),
        P(("blk", "tile"), None),
        P(("blk", "tile"), None),
        P(("blk", "tile"), None),
    )
    out_specs = (P(None, None, None, ("blk", "tile")), P(None, ("blk", "tile")))
    return jax.shard_map(shards, mesh=mesh, in_specs=in_specs, out_specs=out_specs, check_vma=False)
```

```python
import functools

import jax
import jax.numpy as jnp
from jax import lax
from jax.experimental import pallas as pl
from jax.experimental.pallas import tpu as pltpu
from jax.sharding import PartitionSpec as P

DIRS = 6
BANDS = 2
HOURS = 48
NY = 4
NZ = 8
NT = NY * NZ
NB = 8
CUT = 4
DIR_WEIGHTS = (0.06, 0.06, 0.22, 0.22, 0.22, 0.22)
SHORT_FACTOR = 0.7 / 0.97
MESH = pl.DeviceIdType.MESH
RAD_ROWS = 112
FIRST_SENDS = 12
LOW_PER_COLUMN = 2
UNROLL = 8
LATE_LANE = 64
NEAR_AFTER = 1


def entry_slots(flat_mask, flat_source, tracer_count):
    tracer_ids = jnp.arange(tracer_count, dtype=jnp.int32)
    matching = (flat_source[:, None] == tracer_ids[None, :]).astype(jnp.int32)
    counted = matching * flat_mask[:, None]
    earlier = jnp.cumsum(counted, axis=0) - counted
    return jnp.sum(earlier * matching, axis=1)


def general(
    facet_temp,
    emissivity,
    longwave_in,
    albedo,
    shortwave_in,
    dir_share,
    view_blocks,
    vis_list,
    vis_mask,
    vis_source,
):
    long_rad = emissivity[None] * facet_temp**4 + (1.0 - emissivity[None]) * longwave_in
    short_rad = albedo[None] * shortwave_in
    radiosity = jnp.stack([long_rad, short_rad], 0).astype(jnp.bfloat16)
    local = jnp.concatenate(
        [radiosity.reshape(BANDS * HOURS, -1), dir_share.reshape(DIRS, -1)], axis=0
    )
    copies = jnp.broadcast_to(local[None], (lax.axis_size("blk"),) + local.shape)
    strip = lax.all_to_all(copies, "blk", split_axis=0, concat_axis=0, tiled=True)
    strip = jnp.transpose(strip, (1, 0, 2)).reshape(local.shape[0], -1).astype(jnp.float32)
    product = strip[BANDS * HOURS :, None, :] * strip[None, : BANDS * HOURS]
    strip_rows = product.astype(jnp.bfloat16).reshape(DIRS * BANDS * HOURS, -1)
    tracer_count = lax.axis_size("tile")
    capacity = view_blocks.shape[3]
    block_facets = view_blocks.shape[4]
    tile_points = view_blocks.shape[5]
    outgoing = view_blocks.reshape(tracer_count, capacity, block_facets, tile_points)
    received = lax.all_to_all(outgoing, "tile", split_axis=0, concat_axis=0, tiled=True)
    tiles_here, slot_count = vis_list.shape
    flat_mask = vis_mask.reshape(-1)
    flat_source = vis_source.reshape(-1)
    position = jnp.minimum(entry_slots(flat_mask, flat_source, tracer_count), capacity - 1)
    pick_index = flat_source * capacity + position
    blocks = received.reshape(tracer_count * capacity, block_facets, tile_points)[pick_index]
    blocks = blocks * flat_mask.astype(jnp.bfloat16)[:, None, None]
    blocks = blocks.reshape(tiles_here, slot_count * block_facets, tile_points)
    columns = strip_rows.shape[0]
    strip_blocks = strip_rows.reshape(columns, -1, block_facets)

    def one_tile(tile_args):
        tile_ids, tile_blocks = tile_args
        facet_rows = jnp.take(strip_blocks, tile_ids, axis=1).reshape(
            columns, slot_count * block_facets
        )
        return jnp.dot(facet_rows, tile_blocks, preferred_element_type=jnp.float32)

    per_tile = lax.map(one_tile, (vis_list, blocks))
    flux = jnp.transpose(per_tile, (1, 0, 2)).reshape(columns, tiles_here * tile_points)
    return flux


def within(index, size):
    return jnp.minimum(jnp.maximum(index, 0), size - 1)


def column_of(x):
    rows, width = x.shape
    eye = lax.broadcasted_iota(jnp.int32, (width, width), 0) == lax.broadcasted_iota(
        jnp.int32, (width, width), 1
    )
    parts = []
    for i in range(rows):
        line = jnp.broadcast_to(x[i : i + 1, :].astype(jnp.float32), (width, width))
        parts.append(jnp.sum(jnp.where(eye, line, 0.0), axis=1, keepdims=True))
    return jnp.concatenate(parts, axis=0)


def fill_flag(mask_ref, source_ref, flag):
    mask = column_of(mask_ref[...])
    source = column_of(source_ref[...])
    lane = lax.broadcasted_iota(jnp.int32, (mask.shape[0], 128), 1).astype(jnp.float32)
    named = jnp.sum(jnp.where((mask > 0.5) & (source == lane), 1.0, 0.0), axis=0, keepdims=True)
    most = jnp.max(named, axis=1, keepdims=True)
    flag[...] = jnp.broadcast_to(jnp.where(most > CUT + 0.5, 1, 0), flag.shape).astype(jnp.int32)


def fill_tables(last_row, list_ref, mask_ref, source_ref, table, ends):
    entries = mask_ref.shape[0] * mask_ref.shape[1]
    slots = mask_ref.shape[1]
    ids = column_of(list_ref[...])
    mask = column_of(mask_ref[...])
    source = column_of(source_ref[...])
    used = mask > 0.5
    entry = lax.broadcasted_iota(jnp.int32, (entries, 1), 0)
    tile = (entry // slots).astype(jnp.float32)
    before = (
        lax.broadcasted_iota(jnp.int32, (entries, entries), 1)
        < lax.broadcasted_iota(jnp.int32, (entries, entries), 0)
    ).astype(jnp.bfloat16)
    lane = lax.broadcasted_iota(jnp.int32, (entries, 128), 1).astype(jnp.float32)

    def earlier(chosen):
        count = jnp.dot(before, chosen.astype(jnp.bfloat16), preferred_element_type=jnp.float32)
        return jnp.sum(count * chosen, axis=1, keepdims=True)

    by_source = jnp.where(used & (source == lane), 1.0, 0.0)
    position = earlier(by_source)
    first = (last_row * NZ).astype(jnp.float32)
    late = (position == float(CUT - 1)) & (source >= first) & (source < first + float(NZ))
    group = jnp.where(late, float(2 * CUT), position)
    by_group = jnp.where(used & (group == lane), 1.0, 0.0)
    rank = earlier(by_group)
    place = jnp.where(late, float(CUT * NT - NZ), position * NT) + rank
    wide = lax.broadcasted_iota(jnp.int32, (entries, entries), 1).astype(jnp.float32)
    at = jnp.where(used & (place == wide), 1.0, 0.0)
    table[...] = jnp.zeros_like(table)
    table[0:1, :] = jnp.sum(at * ids, axis=0, keepdims=True).astype(jnp.int32)
    table[1:2, :] = jnp.sum(at * source, axis=0, keepdims=True).astype(jnp.int32)
    table[2:3, :] = jnp.sum(at * tile, axis=0, keepdims=True).astype(jnp.int32)
    up_to = jnp.where(tile <= lane, 1.0, 0.0)
    up_to_late = jnp.where(tile <= lane - LATE_LANE, 1.0, 0.0)
    for p in range(2 * CUT):
        chosen = jnp.sum(jnp.where(lane == float(p), by_group, 0.0), axis=1, keepdims=True)
        line = chosen * up_to
        if p == CUT - 1:
            chosen = jnp.sum(jnp.where(lane == float(2 * CUT), by_group, 0.0), axis=1, keepdims=True)
            line = jnp.where(lane < float(LATE_LANE), line, chosen * up_to_late)
        ends[p : p + 1, :] = jnp.sum(line, axis=0, keepdims=True).astype(jnp.int32)


def kernel(
    view, temp_hbm, emis_hbm, longwave_hbm, albedo_hbm, short_hbm, share_hbm, list_hbm, mask_hbm, source_hbm,
    flux_out, bad,
    low0, low1, low2, low3, low_late, high, near, rad, rows, running, table, ends, flag, flags, sums, pick, over, overs,
    table_s, ends_s, pick_s,
    low_send, low_recv, ring_send, ring_recv, col_send, col_recv, rad_send, rad_recv,
    flag_send, flag_recv, over_send, over_recv, local, row_here,
    temp_in, emis, longwave, albedo, short, share, list_ref, mask_ref, source_ref, loads,
    flux, flux_sem,
):
    b = lax.axis_index("blk")
    t = lax.axis_index("tile")
    y = t // NZ
    z = lax.rem(t, NZ)

    def tile_peer(i):
        j = lax.rem(i, NZ)
        odd = lax.rem(j, 2)
        half = NZ // 2
        dz = odd * (half + j // 2) + (1 - odd) * (half - j // 2) * ((j + NZ - 1) // NZ)
        return lax.rem(y + i // NZ, NY) * NZ + lax.rem(z + dz, NZ)

    barrier = pltpu.get_barrier_semaphore()

    for i in range(1, NZ):
        pl.semaphore_signal(barrier, inc=1, device_id=(b, tile_peer(i)), device_id_type=MESH)
    for i in range(NZ, NT, NZ):
        pl.semaphore_signal(barrier, inc=1, device_id=(b, tile_peer(i)), device_id_type=MESH)
    for i in range(1, NB):
        pl.semaphore_signal(
            barrier, inc=1, device_id=(lax.rem(b + i, NB), t), device_id_type=MESH
        )

    loading = [
        pltpu.make_async_copy(src, dst, loads.at[n])
        for n, (src, dst) in enumerate(
            (
                (temp_hbm, temp_in),
                (emis_hbm, emis),
                (longwave_hbm, longwave),
                (albedo_hbm, albedo),
                (short_hbm, short),
                (share_hbm, share),
                (list_hbm, list_ref),
                (mask_hbm, mask_ref),
                (source_hbm, source_ref),
            )
        )
    ]
    for n in (7, 8, 0, 1, 2, 3, 4, 5, 6):
        loading[n].start()
    high_copy = pltpu.make_async_copy(view.at[:, pl.ds(CUT, CUT)], high, local.at[0])
    low = (low0, low1, low2, low3)
    own_copies = [
        pltpu.make_async_copy(view.at[t, p], low[p].at[t], local.at[5 + p]) for p in range(CUT)
    ]

    loading[7].wait()
    loading[8].wait()
    fill_flag(mask_ref, source_ref, flag)
    flags[z] = flag[...]

    pl.semaphore_wait(barrier, NZ - 1 + NY - 1 + NB - 1)
    for i in range(NZ, NT, NZ):
        pl.semaphore_signal(row_here, inc=1, device_id=(b, tile_peer(i)), device_id_type=MESH)

    def flag_to(i):
        return pltpu.make_async_remote_copy(
            src_ref=flag, dst_ref=flags.at[z], send_sem=flag_send.at[i], recv_sem=flag_recv.at[i],
            device_id=(b, tile_peer(i)), device_id_type=MESH,
        )

    def sums_to(i):
        return pltpu.make_async_remote_copy(
            src_ref=sums.at[y], dst_ref=sums.at[y],
            send_sem=flag_send.at[NZ + i], recv_sem=flag_recv.at[NZ + i],
            device_id=(b, tile_peer(i * NZ)), device_id_type=MESH,
        )

    def rad_to(i):
        return pltpu.make_async_remote_copy(
            src_ref=rad.at[b], dst_ref=rad.at[b], send_sem=rad_send.at[i], recv_sem=rad_recv.at[i],
            device_id=(lax.rem(b + i, NB), t), device_id_type=MESH,
        )

    def low_to(p, i, late=False):
        return pltpu.make_async_remote_copy(
            src_ref=view.at[tile_peer(i), p], dst_ref=low_late.at[z] if late else low[p].at[t],
            send_sem=low_send.at[p, i], recv_sem=low_recv.at[p, i],
            device_id=(b, tile_peer(i)), device_id_type=MESH,
        )

    def over_to(i):
        return pltpu.make_async_remote_copy(
            src_ref=over, dst_ref=overs.at[b], send_sem=over_send.at[i], recv_sem=over_recv.at[i],
            device_id=(lax.rem(b + i, NB), t), device_id_type=MESH,
        )

    def ring_to(way, step):
        toward = lax.rem(z + (1, NZ - 1)[way], NZ)
        behind = y * NZ + lax.rem(z + (NZ - step, step)[way], NZ)
        half = CUT // 2
        part = pl.ds(0, CUT) if step < NZ // 2 - 1 else pl.ds(way * half, half)
        return pltpu.make_async_remote_copy(
            src_ref=near.at[behind, part], dst_ref=near.at[behind, part],
            send_sem=ring_send.at[way, step], recv_sem=ring_recv.at[way, step],
            device_id=(b, y * NZ + toward), device_id_type=MESH,
        )

    def column_to(dy, dz):
        held = y * NZ + lax.rem(z + dz, NZ)
        return pltpu.make_async_remote_copy(
            src_ref=near.at[held], dst_ref=near.at[held],
            send_sem=col_send.at[dy, dz], recv_sem=col_recv.at[dy, dz],
            device_id=(b, lax.rem(y + dy, NY) * NZ + z), device_id_type=MESH,
        )

    def looped(lo, hi, action):
        def body(i, carry):
            action(i)
            return carry

        lax.fori_loop(lo, hi, body, 0)

    sent = [1]

    def send_low(count):
        k = sent[0]
        end = min(CUT * NT, k + count)
        while k < end:
            p = k // NT
            stop = min(end, (p + 1) * NT)
            lo, hi = max(k - p * NT, 1), stop - p * NT
            split = NT - NZ if p == CUT - 1 else NT
            if lo < split:
                looped(lo, min(hi, split), lambda i: low_to(p, i).start())
            if hi > split:
                looped(max(lo, split), hi, lambda i: low_to(p, i, True).start())
            k = stop
        sent[0] = k

    for i in range(1, NZ):
        flag_to(i).start()
    send_low(NZ - 1)
    high_copy.start()
    pl.semaphore_wait(row_here, NY - 1)
    send_low(FIRST_SENDS // 2)

    for copy in loading[:7]:
        copy.wait()
    emissivity = emis[...]
    long_rad = emissivity * temp_in[:, 0, :] ** 4 + (1.0 - emissivity) * longwave[:, 0, :]
    rad[b, 0:HOURS, :] = long_rad.astype(jnp.bfloat16)
    rad[b, HOURS : 2 * HOURS, :] = (albedo[...] * short[:, 0, :]).astype(jnp.bfloat16)
    rad[b, 2 * HOURS : RAD_ROWS, :] = jnp.concatenate(
        [share[...].astype(jnp.float32), jnp.zeros((RAD_ROWS - 2 * HOURS - DIRS, share.shape[1]), jnp.float32)],
        axis=0,
    ).astype(jnp.bfloat16)

    for i in range(1, NZ):
        flag_to(i).wait()
    total = jnp.zeros((8, 128), jnp.int32)
    where_to = jnp.zeros((8, 128), jnp.int32)
    for o in range(NZ):
        total += flags[o]
        where_to += flags[o] * (y * NZ + o)
    sums[y, 0] = total
    sums[y, 1] = where_to
    for i in range(1, NY):
        sums_to(i).start()
    send_low(FIRST_SENDS // 2)
    looped(1, NB, lambda i: rad_to(i).start())
    for i in range(1, NY):
        sums_to(i).wait()
    total = sums[0, 0]
    where_to = sums[0, 1]
    for i in range(1, NY):
        total += sums[i, 0]
        where_to += sums[i, 1]
    pick[...] = jnp.where(total == 1, where_to, 0)
    over[...] = jnp.where(total > 1, 1, 0).astype(jnp.int32)
    overs[b] = over[...]
    pick_copy = pltpu.make_async_copy(pick, pick_s, local.at[4])
    pick_copy.start()
    looped(1, NB, lambda i: over_to(i).start())
    high_copy.wait()
    pick_copy.wait()
    near[t] = high[within(pick_s[0, 0], NT)]
    for copy in own_copies:
        copy.start()

    for step in range(NZ // 2):
        ring_to(0, step).start()
        ring_to(1, step).start()
        if step == 0:
            shares = [0]
        else:
            shares = [step, NZ - step]
        for dz in shares:
            for dy in range(1, NY):
                column_to(dy, dz).start()
                send_low(LOW_PER_COLUMN)
        ring_to(0, step).wait()
        ring_to(1, step).wait()
    for dy in range(1, NY):
        column_to(dy, NZ // 2).start()
        send_low(LOW_PER_COLUMN)
    send_low(CUT * NT)

    running[0] = jnp.zeros(running.shape[1:], jnp.float32)
    fill_tables(lax.rem(y + 1, NY), list_ref, mask_ref, source_ref, table, ends)
    table_copy = pltpu.make_async_copy(table, table_s, local.at[2])
    table_copy.start()
    ends_copy = pltpu.make_async_copy(ends, ends_s, local.at[3])
    ends_copy.start()
    for copy in own_copies:
        copy.wait()
    table_copy.wait()
    ends_copy.wait()
    looped(1, NB, lambda i: rad_to(i).wait())

    facet_blocks = rad.shape[2] // 128

    def weight(j, carry):
        for q in range(facet_blocks):
            cols = slice(q * 128, (q + 1) * 128)
            radiosity = rad[j, 0 : 2 * HOURS, cols].astype(jnp.float32)
            shares = rad[j, 2 * HOURS : RAD_ROWS, cols].astype(jnp.float32)
            for d in range(DIRS):
                rows[j * facet_blocks + q, d * 2 * HOURS : (d + 1) * 2 * HOURS, :] = (
                    shares[d : d + 1, :] * radiosity
                ).astype(jnp.bfloat16)
        return carry

    lax.fori_loop(0, NB, weight, 0)

    tiles = mask_ref.shape[0]

    def tile_out(i):
        cols = pl.ds(i * 128, 128)
        return pltpu.make_async_copy(flux.at[:, cols], flux_out.at[:, cols], flux_sem.at[i])

    def group_products(p, base, count, held, first_phase, lane=0):
        def body(turn, carry):
            for u in range(UNROLL):
                r = turn * UNROLL + u
                g = base + r
                same = (r > 0) & (table_s[2, g] == table_s[2, jnp.maximum(g - 1, 0)])
                product = jnp.dot(
                    rows[within(table_s[0, g], rows.shape[0])],
                    held(within(table_s[1, g], NT)),
                    preferred_element_type=jnp.float32,
                )
                running[r + 1] = product + jnp.where(same, running[r], 0.0)
            return carry

        lax.fori_loop(0, count // UNROLL, body, 0)
        for i in range(tiles):
            end = within(ends_s[p, lane + i], NT + 1)
            start = within(ends_s[p, lane + i - 1], NT + 1) if i else 0
            cols = slice(i * 128, (i + 1) * 128)
            part = jnp.where(end > start, running[end], 0.0)
            if first_phase:
                flux[:, cols] = part
            else:
                flux[:, cols] += part
            if lane:
                tile_out(i).start()

    def low_wait(p, lo, hi, late=False):
        looped(lo, hi, lambda i: low_to(p, i, late).wait())

    def near_products():
        for dy in range(1, NY):
            looped(0, NZ, lambda dz: column_to(dy, dz).wait())
        for q in range(CUT):
            group_products(CUT + q, (CUT + q) * NT, NT, lambda s: near[s, q], False)

    looped(1, NB, lambda i: over_to(i).wait())
    any_over = overs[0]
    for i in range(1, NB):
        any_over += overs[i]
    over[...] = any_over
    over_copy = pltpu.make_async_copy(over, pick_s, local.at[4])
    over_copy.start()
    over_copy.wait()
    bad[0, 0] = pick_s[0, 0]

    for p in range(CUT - 1):
        low_wait(p, 1, NT)
        group_products(p, p * NT, NT, lambda s: low[p][s], p == 0)
        if p == NEAR_AFTER:
            near_products()
    p = CUT - 1
    low_wait(p, 1, NT - NZ)
    group_products(p, p * NT, NT - NZ, lambda s: low[p][s], False)
    low_wait(p, NT - NZ, NT, True)
    group_products(p, CUT * NT - NZ, NZ, lambda s: low_late[lax.rem(s, NZ)], False, LATE_LANE)
    for i in range(tiles):
        tile_out(i).wait()


def finish(found, flux, radiant):
    total = None
    for d in range(DIRS):
        base = d * 2 * HOURS
        part = DIR_WEIGHTS[d] * (
            found[base : base + HOURS, :] + SHORT_FACTOR * found[base + HOURS : base + 2 * HOURS, :]
        )
        total = part if total is None else total + part
    radiant[...] = jnp.sqrt(jnp.sqrt(total))
    flux[...] = found[...]


def shards(*args):
    (facet_temp, emissivity, longwave_in, albedo, shortwave_in, dir_share, view_blocks,
     vis_list, vis_mask, vis_source) = args
    width = facet_temp.shape[2]
    capacity, facets, points = view_blocks.shape[3:]
    tiles, slots = vis_list.shape
    columns = DIRS * BANDS * HOURS
    assert capacity == 2 * CUT and tiles * slots == capacity * NT
    view = view_blocks.reshape(NT, capacity, facets, points)
    operands = (
        facet_temp,
        emissivity,
        longwave_in,
        albedo,
        shortwave_in,
        dir_share.reshape(DIRS, width),
        vis_list,
        vis_mask,
        vis_source,
    )
    dma = pltpu.SemaphoreType.DMA
    found, bad = pl.pallas_call(
        kernel,
        out_shape=(
            jax.ShapeDtypeStruct((columns, tiles * points), jnp.float32),
            jax.ShapeDtypeStruct((1, 1), jnp.int32),
        ),
        in_specs=[pl.BlockSpec(memory_space=pl.ANY)] * 10,
        out_specs=(pl.BlockSpec(memory_space=pl.ANY), pl.BlockSpec(memory_space=pltpu.SMEM)),
        scratch_shapes=[
            *([pltpu.VMEM((NT, facets, points), jnp.bfloat16)] * CUT),
            pltpu.VMEM((NZ, facets, points), jnp.bfloat16),
            pltpu.VMEM((NT, CUT, facets, points), jnp.bfloat16),
            pltpu.VMEM((NT, CUT, facets, points), jnp.bfloat16),
            pltpu.VMEM((NB, RAD_ROWS, width), jnp.bfloat16),
            pltpu.VMEM((NB * width // facets, columns, facets), jnp.bfloat16),
            pltpu.VMEM((NT + 1, columns, points), jnp.float32),
            pltpu.VMEM((8, tiles * slots), jnp.int32),
            pltpu.VMEM((8, 128), jnp.int32),
            pltpu.VMEM((8, 128), jnp.int32),
            pltpu.VMEM((NZ, 8, 128), jnp.int32),
            pltpu.VMEM((NY, 2, 8, 128), jnp.int32),
            pltpu.VMEM((8, 128), jnp.int32),
            pltpu.VMEM((8, 128), jnp.int32),
            pltpu.VMEM((NB, 8, 128), jnp.int32),
            pltpu.SMEM((8, tiles * slots), jnp.int32),
            pltpu.SMEM((8, 128), jnp.int32),
            pltpu.SMEM((8, 128), jnp.int32),
            dma((CUT, NT)),
            dma((CUT, NT)),
            dma((2, NZ // 2)),
            dma((2, NZ // 2)),
            dma((NY, NZ)),
            dma((NY, NZ)),
            dma((NB,)),
            dma((NB,)),
            dma((NT,)),
            dma((NT,)),
            dma((NB,)),
            dma((NB,)),
            dma((5 + CUT,)),
            pltpu.SemaphoreType.REGULAR,
            *[pltpu.VMEM(x.shape, x.dtype) for x in operands],
            dma((len(operands),)),
            pltpu.VMEM((columns, tiles * points), jnp.float32),
            dma((tiles,)),
        ],
        compiler_params=pltpu.CompilerParams(
            collective_id=0, has_side_effects=True, vmem_limit_bytes=55 * 1024 * 1024
        ),
    )(view, *operands)
    found = lax.cond(bad[0, 0] > 0, lambda: general(*args), lambda: found)
    width_out = 4 * points
    flux, radiant = pl.pallas_call(
        finish,
        grid=(tiles // 4,),
        out_shape=(
            jax.ShapeDtypeStruct((columns, tiles * points), jnp.float32),
            jax.ShapeDtypeStruct((HOURS, tiles * points), jnp.float32),
        ),
        in_specs=[pl.BlockSpec((columns, width_out), lambda i: (0, i))],
        out_specs=(
            pl.BlockSpec((columns, width_out), lambda i: (0, i)),
            pl.BlockSpec((HOURS, width_out), lambda i: (0, i)),
        ),
    )(found)
    return flux.reshape(DIRS, BANDS, HOURS, tiles * points), radiant


def solution(mesh):
    in_specs = (
        P(None, "tile", "blk"),
        P("tile", "blk"),
        P(None, "tile", "blk"),
        P("tile", "blk"),
        P(None, "tile", "blk"),
        P(None, "tile", "blk"),
        P("blk", "tile", None, None, None, None),
        P(("blk", "tile"), None),
        P(("blk", "tile"), None),
        P(("blk", "tile"), None),
    )
    out_specs = (P(None, None, None, ("blk", "tile")), P(None, ("blk", "tile")))
    return jax.shard_map(shards, mesh=mesh, in_specs=in_specs, out_specs=out_specs, check_vma=False)
```
